32 devices in a mesh: dp: 16 (over z, y, core), tensor: 2 (over x).
Axes of the slice: x: 2, y: 2, z: 4, core: 2. Of those that a mesh axis runs over, the one named last changes fastest.
Arguments:
- tokens: bfloat16 [16384, 2048], P(('dp', 'tensor')), may hold values from -6 to 6
- cotangent: bfloat16 [16384, 2048], P(('dp', 'tensor')), may hold values from -6 to 6
- lengths: int32 [16], P('dp'), may hold values from 640 to 1024, as said below
- w_query: float32 [2048, 2048], P('dp', 'tensor'), may hold values from -0.125 to 0.125
- query_mean: float32 [2048, 2048], P('dp', 'tensor'), may hold values from -80 to 80
- query_square: float32 [2048, 2048], P('dp', 'tensor'), may hold values from 655.36 to 2621.44
- w_keyval: float32 [2048, 2, 1024], P('dp', None, 'tensor'), may hold values from -0.125 to 0.125
- keyval_mean: float32 [2048, 2, 1024], P('dp', None, 'tensor'), may hold values from -80 to 80
- keyval_square: float32 [2048, 2, 1024], P('dp', None, 'tensor'), may hold values from 655.36 to 2621.44
- w_out: float32 [2048, 2048], P('tensor', 'dp'), may hold values from -2 to 2
- out_mean: float32 [2048, 2048], P('tensor', 'dp'), may hold values from -5 to 5
- out_square: float32 [2048, 2048], P('tensor', 'dp'), may hold values from 2.72 to 10.88
- w_gateup: float32 [2048, 2, 6144], P('dp', None, 'tensor'), may hold values from -0.125 to 0.125
- gateup_mean: float32 [2048, 2, 6144], P('dp', None, 'tensor'), may hold values from -28 to 28
- gateup_square: float32 [2048, 2, 6144], P('dp', None, 'tensor'), may hold values from 81.92 to 327.68
- w_down: float32 [6144, 2048], P('tensor', 'dp'), may hold values from -0.078125 to 0.078125
- down_mean: float32 [6144, 2048], P('tensor', 'dp'), may hold values from -48 to 48
- down_square: float32 [6144, 2048], P('tensor', 'dp'), may hold values from 245.76 to 983.04
- norm_gains: float32 [2, 2048], replicated, may hold values from 0.5 to 1.5
- norm_mean: float32 [2, 2048], replicated, may hold values from -80 to 80
- norm_square: float32 [2, 2048], replicated, may hold values from 819.2 to 3276.8
- head_gains: float32 [2, 128], replicated, may hold values from 0.5 to 1.5
- head_mean: float32 [2, 128], replicated, may hold values from -320 to 320
- head_square: float32 [2, 128], replicated, may hold values from 13107.2 to 52428.8
Outputs:
- layer_out: float32 [16384, 2048], P(('dp', 'tensor'))
- tokens_grad: float32 [16384, 2048], P(('dp', 'tensor'))
- query_next: float32 [2048, 2048], P('dp', 'tensor')
- query_mean_next: float32 [2048, 2048], P('dp', 'tensor')
- query_square_next: float32 [2048, 2048], P('dp', 'tensor')
- keyval_next: float32 [2048, 2, 1024], P('dp', None, 'tensor')
- keyval_mean_next: float32 [2048, 2, 1024], P('dp', None, 'tensor')
- keyval_square_next: float32 [2048, 2, 1024], P('dp', None, 'tensor')
- out_next: float32 [2048, 2048], P('tensor', 'dp')
- out_mean_next: float32 [2048, 2048], P('tensor', 'dp')
- out_square_next: float32 [2048, 2048], P('tensor', 'dp')
- gateup_next: float32 [2048, 2, 6144], P('dp', None, 'tensor')
- gateup_mean_next: float32 [2048, 2, 6144], P('dp', None, 'tensor')
- gateup_square_next: float32 [2048, 2, 6144], P('dp', None, 'tensor')
- down_next: float32 [6144, 2048], P('tensor', 'dp')
- down_mean_next: float32 [6144, 2048], P('tensor', 'dp')
- down_square_next: float32 [6144, 2048], P('tensor', 'dp')
- norm_next: float32 [2, 2048], replicated
- norm_mean_next: float32 [2, 2048], replicated
- norm_square_next: float32 [2, 2048], replicated
- head_next: float32 [2, 128], replicated
- head_mean_next: float32 [2, 128], replicated
- head_square_next: float32 [2, 128], replicated
The draws below stay inside these ranges and needn't reach their ends.
Inputs may be any that keep to these rules, and one draw needn't show every extreme that they name: Group g holds one sequence of lengths[g] tokens from its first row, the rest of its 1024 rows are padding; in every draw some group's sequence fills all 1024 rows.
All inputs are finite; a program needn't handle non-finite values.
Results may differ from the reference program's by a relative error of at most 0.015.
Values may be sent and summed in bfloat16 or wider, within the bound.
No kernel may reach another device: no remote copies, remote signals or barrier semaphores. Data moves between devices by JAX's collectives and lax.ppermute only.
A program may use at most 320 MiB of HBM per device.

```python
import math
import jax
import jax.numpy as jnp
from jax import lax

D = 2048
HEADS = 16
KVH = 8
HD = 128
FF = 6144
STEP = 10
CAP = 1024
LEN_MIN = 640
GROUPS = 16
TOKENS = 16384
QD = 2048
KVD = 1024


def draw_lengths(key, part):
    key = jax.random.fold_in(key, 11)
    first_key, second_key = jax.random.split(key)
    drawn = jax.random.randint(first_key, (GROUPS,), LEN_MIN, CAP + 1)
    full_at = jax.random.randint(second_key, (), 0, GROUPS)
    return jnp.where(jnp.arange(GROUPS) == full_at, CAP, drawn).astype(jnp.int32)


def level_of(stream_key, shape, shards, least, top_value):
    loudness = 1.0
    for axis_at, parts in shards:
        draws = jax.random.uniform(jax.random.fold_in(jax.random.fold_in(stream_key, 6), axis_at), (parts,), jnp.float32, least / len(shards), top_value / len(shards))
        loudness = loudness * jnp.repeat(jnp.exp(draws), shape[axis_at] // parts).reshape((-1,) + (1,) * (len(shape) - 1 - axis_at))
    return loudness


def noise(stream_key, dims, width, reach, shards=(), dtype=jnp.bfloat16):
    array = width * jax.random.normal(stream_key, dims, jnp.float32)
    if shards:
        array = array * level_of(stream_key, dims, shards, -0.22, 0.18)
    return jnp.clip(array, -reach, reach).astype(dtype)


def setup_inputs(seed: int = 0) -> dict:
    key_of = jax.random.split(jax.random.key(seed), 25)
    return {
        "tokens": noise(key_of[0], (TOKENS, D), 1.0, 6.0, ((0, 32),)),
        "cotangent": noise(key_of[1], (TOKENS, D), 1.0, 6.0, ((0, 32),)),
        "lengths": draw_lengths(jax.random.fold_in(key_of[24], 71), 0),
        "w_query": noise(key_of[3], (D, QD), D ** -0.5, 0.125, ((0, 16), (1, 2)), jnp.float32),
        "query_mean": noise(key_of[4], (D, QD), (0.1 * TOKENS ** 0.5), 80.0, ((0, 16), (1, 2)), jnp.float32),
        "query_square": jnp.clip(jnp.exp(math.log(2621.44) - 1.3862944 * jax.random.uniform(key_of[5], (D, QD), jnp.float32) ** level_of(key_of[5], (D, QD), ((0, 16), (1, 2)), -0.2, 0.2)), 655.36, 2621.44),
        "w_keyval": noise(key_of[6], (D, 2, KVD), D ** -0.5, 0.125, ((0, 16), (2, 2)), jnp.float32),
        "keyval_mean": noise(key_of[7], (D, 2, KVD), (0.1 * TOKENS ** 0.5), 80.0, ((0, 16), (2, 2)), jnp.float32),
        "keyval_square": jnp.clip(jnp.exp(math.log(2621.44) - 1.3862944 * jax.random.uniform(key_of[8], (D, 2, KVD), jnp.float32) ** level_of(key_of[8], (D, 2, KVD), ((0, 16), (2, 2)), -0.2, 0.2)), 655.36, 2621.44),
        "w_out": noise(key_of[9], (QD, D), 8 ** -0.5, 2.0, ((0, 2), (1, 16)), jnp.float32),
        "out_mean": noise(key_of[10], (QD, D), (0.2 * (TOKENS / CAP) ** 0.5), 5.0, ((0, 2), (1, 16)), jnp.float32),
        "out_square": jnp.clip(jnp.exp(math.log(10.88) - 1.3862944 * jax.random.uniform(key_of[11], (QD, D), jnp.float32) ** level_of(key_of[11], (QD, D), ((0, 2), (1, 16)), -0.2, 0.2)), 2.72, 10.88),
        "w_gateup": noise(key_of[12], (D, 2, FF), D ** -0.5, 0.125, ((0, 16), (2, 2)), jnp.float32),
        "gateup_mean": noise(key_of[13], (D, 2, FF), (0.035 * TOKENS ** 0.5), 28.0, ((0, 16), (2, 2)), jnp.float32),
        "gateup_square": jnp.clip(jnp.exp(math.log(327.68) - 1.3862944 * jax.random.uniform(key_of[14], (D, 2, FF), jnp.float32) ** level_of(key_of[14], (D, 2, FF), ((0, 16), (2, 2)), -0.2, 0.2)), 81.92, 327.68),
        "w_down": noise(key_of[15], (FF, D), FF ** -0.5, 0.078125, ((0, 2), (1, 16)), jnp.float32),
        "down_mean": noise(key_of[16], (FF, D), (0.06 * TOKENS ** 0.5), 48.0, ((0, 2), (1, 16)), jnp.float32),
        "down_square": jnp.clip(jnp.exp(math.log(983.04) - 1.3862944 * jax.random.uniform(key_of[17], (FF, D), jnp.float32) ** level_of(key_of[17], (FF, D), ((0, 2), (1, 16)), -0.2, 0.2)), 245.76, 983.04),
        "norm_gains": jnp.clip(1.0 + 0.1 * jax.random.normal(key_of[18], (2, D), jnp.float32), 0.5, 1.5),
        "norm_mean": noise(key_of[19], (2, D), (0.11 * TOKENS ** 0.5), 80.0, (), jnp.float32),
        "norm_square": jnp.clip(jnp.exp(jax.random.uniform(key_of[20], (2, D), jnp.float32, math.log(819.2), math.log(3276.8))), 819.2, 3276.8),
        "head_gains": jnp.clip(1.0 + 0.1 * jax.random.normal(key_of[21], (2, HD), jnp.float32), 0.5, 1.5),
        "head_mean": noise(key_of[22], (2, HD), (0.11 * (TOKENS * HEADS) ** 0.5), 320.0, (), jnp.float32),
        "head_square": jnp.clip(jnp.exp(jax.random.uniform(key_of[23], (2, HD), jnp.float32, math.log(13107.2), math.log(52428.8))), 13107.2, 52428.8),
    }


@jax.custom_vjp
def low(v):
    return lax.optimization_barrier(v.astype(jnp.bfloat16)).astype(jnp.float32)

@jax.custom_vjp
def low_back(v):
    return v

def low_keep(v):
    return (low(v), None)

def low_pass(kept, grad):
    return (grad,)

def back_keep(v):
    return (v, None)

def back_low(kept, grad):
    return (low(grad),)
low.defvjp(low_keep, low_pass)
low_back.defvjp(back_keep, back_low)
EPS_NORM = 1e-06
ROPE_BASE = 1000000.0
BETA_ONE = 0.9
BETA_TWO = 0.95
ADAM_EPS = 1e-08
WEIGHT_DECAY = 0.1
RATE_SCALE = 2.0
GAIN_RATE = 0.6
OUT_FAN = 8.0
PRECISE = lax.Precision.HIGHEST

def rms_norm(values, gain_vec):
    return values * lax.rsqrt(lax.optimization_barrier(jnp.mean(values * values, axis=-1, keepdims=True)) + EPS_NORM) * gain_vec

def rope_tables(row_count):
    places = jnp.arange(row_count).astype(jnp.float32)
    inverse_freq = ROPE_BASE ** (-(jnp.arange(HD // 2).astype(jnp.float32) * 2.0) / HD)
    angles = places[:, None] * inverse_freq[None, :]
    angles = jnp.concatenate([angles, angles], axis=1)
    return (jnp.cos(angles)[:, None, :], jnp.sin(angles)[:, None, :])

def rotate(values, cosine, sine_part):
    half_size = values.shape[-1] // 2
    turned = jnp.concatenate([-values[..., half_size:], values[..., :half_size]], axis=-1)
    return values * cosine + turned * sine_part

def layer_rows(stream, length, query_low, keyval_low, out_low, gateup_low, down_low, norm_gains, head_gains):
    cap_rows = stream.shape[0]
    normed_one = low(rms_norm(stream, norm_gains[0]))
    queries = low_back(jnp.dot(normed_one, query_low, precision=PRECISE))
    keyvals = low_back(jnp.einsum('td,dsk->tsk', normed_one, keyval_low, precision=PRECISE))
    cosine, sine_part = rope_tables(cap_rows)
    queries = queries.reshape(cap_rows, HEADS, HD)
    key_part = keyvals[:, 0].reshape(cap_rows, KVH, HD)
    value_low = low(keyvals[:, 1].reshape(cap_rows, KVH, HD))
    query_turned = low(rotate(rms_norm(queries, head_gains[0]), cosine, sine_part))
    key_turned = low(rotate(rms_norm(key_part, head_gains[1]), cosine, sine_part))
    query_group = query_turned.reshape(cap_rows, KVH, HEADS // KVH, HD)
    scores = low_back(jnp.einsum('tngh,snh->ngts', query_group, key_turned, precision=PRECISE)) * HD ** (-0.5)
    places = jnp.arange(cap_rows)
    allowed = (places[None, :] <= places[:, None]) & (places[None, :] < length)
    scores = jnp.where(allowed, scores, -1e+30)
    chances = low(jax.nn.softmax(scores, axis=-1))
    attended = jnp.einsum('ngts,snh->tngh', chances, value_low, precision=PRECISE).reshape(cap_rows, QD)
    attended = low(low_back(attended))
    middle = stream + low_back(jnp.dot(attended, out_low, precision=PRECISE))
    second = low(rms_norm(middle, norm_gains[1]))
    gate_up = low_back(jnp.einsum('td,dsf->tsf', second, gateup_low, precision=PRECISE))
    hidden = low(jax.nn.silu(gate_up[:, 0]) * gate_up[:, 1])
    return middle + low_back(jnp.dot(hidden, down_low, precision=PRECISE))

def adam_step(weight, mean_old, square, gradient, step_rate, decay_rate):
    new_mean = BETA_ONE * mean_old + (1.0 - BETA_ONE) * gradient
    new_square = BETA_TWO * square + (1.0 - BETA_TWO) * gradient * gradient
    fix_one = 1.0 - BETA_ONE ** STEP
    fix_two = 1.0 - BETA_TWO ** STEP
    update = new_mean / fix_one / (jnp.sqrt(new_square / fix_two) + ADAM_EPS)
    return (weight - step_rate * (update + decay_rate * weight), new_mean, new_square)

def reference(tokens, cotangent, lengths, w_query, query_mean, query_square, w_keyval, keyval_mean, keyval_square, w_out, out_mean, out_square, w_gateup, gateup_mean, gateup_square, w_down, down_mean, down_square, norm_gains, norm_mean, norm_square, head_gains, head_mean, head_square):
    stream = tokens.astype(jnp.float32).reshape(GROUPS, CAP, D)
    live_mask = (jnp.arange(CAP)[None, :] < lengths[:, None]).astype(jnp.float32)
    upstream = cotangent.astype(jnp.float32).reshape(GROUPS, CAP, D) * live_mask[:, :, None]

    def forward(stream, w_query, w_keyval, w_out, w_gateup, w_down, norm_gains, head_gains):
        query_low = low(w_query)
        keyval_low = low(w_keyval)
        out_low = low(w_out)
        gateup_low = low(w_gateup)
        down_low = low(w_down)

        def one_group(sums_in, item):
            return (sums_in, layer_rows(item[0], item[1], query_low, keyval_low, out_low, gateup_low, down_low, norm_gains, head_gains))
        _, outputs = lax.scan(jax.checkpoint(one_group), jnp.zeros((), jnp.float32), (stream, lengths))
        return outputs
    layer_out, pullback = jax.vjp(forward, stream, w_query, w_keyval, w_out, w_gateup, w_down, norm_gains, head_gains)
    d_stream, g_query, g_keyval, g_out, g_gateup, g_down, g_norm, g_head = pullback(upstream)
    wide_rate = RATE_SCALE * D ** (-0.5)
    query_new = adam_step(w_query, query_mean, query_square, g_query, wide_rate, WEIGHT_DECAY)
    keyval_new = adam_step(w_keyval, keyval_mean, keyval_square, g_keyval, wide_rate, WEIGHT_DECAY)
    out_new = adam_step(w_out, out_mean, out_square, g_out, RATE_SCALE * OUT_FAN ** (-0.5), WEIGHT_DECAY)
    gateup_new = adam_step(w_gateup, gateup_mean, gateup_square, g_gateup, wide_rate, WEIGHT_DECAY)
    down_new = adam_step(w_down, down_mean, down_square, g_down, RATE_SCALE * FF ** (-0.5), WEIGHT_DECAY)
    norm_new = adam_step(norm_gains, norm_mean, norm_square, g_norm, GAIN_RATE, 0.0)
    head_new = adam_step(head_gains, head_mean, head_square, g_head, GAIN_RATE, 0.0)
    return (layer_out.reshape(TOKENS, D), d_stream.reshape(TOKENS, D), query_new[0], query_new[1], query_new[2], keyval_new[0], keyval_new[1], keyval_new[2], out_new[0], out_new[1], out_new[2], gateup_new[0], gateup_new[1], gateup_new[2], down_new[0], down_new[1], down_new[2], norm_new[0], norm_new[1], norm_new[2], head_new[0], head_new[1], head_new[2])
```

```python
import functools

import jax
import jax.numpy as jnp
from jax import lax
from jax.experimental import pallas as pl
from jax.experimental.pallas import tpu as pltpu
from jax.sharding import Mesh
from jax.sharding import PartitionSpec as P

D = 2048
HD = 128
FF = 6144
STEP = 10
LEN_MIN = 640

EPS_NORM = 1e-06
ROPE_BASE = 1000000.0
BETA_ONE = 0.9
BETA_TWO = 0.95
ADAM_EPS = 1e-08
WEIGHT_DECAY = 0.1
RATE_SCALE = 2.0
GAIN_RATE = 0.6
OUT_FAN = 8.0
LOG2_E = 1.4426950408889634

BF = jnp.bfloat16
F32 = jnp.float32
ROWS = 256
TILE = 256
CHUNKS = 3
WORK = 5 * 10**8

NN = (((1,), (0,)), ((), ()))
NT = (((1,), (1,)), ((), ()))
TN = (((0,), (0,)), ((), ()))


def mm(a, b, dims=NN):
    return lax.dot_general(a, b, dims, preferred_element_type=F32)


class Order:
    def __init__(self, side, length, core):
        one = jnp.ones_like(side)
        self.scalars = jnp.stack([side, 1 - side, length, 0 * one, one, core, 1 - core]).astype(jnp.int32)

    def call(self, kernel, grid, ins, outs, operands, *, after=(), through=(), vmem=48, scratch=(), work, name):
        count, later, made = len(ins), len(after) + len(through), len(outs)
        anywhere = pl.BlockSpec(memory_space=pl.ANY)

        def run(scalars, *refs):
            first = count + later
            token = refs[first + made]
            for i in range(token.shape[0]):
                token[i] = scalars[i]
            kernel(scalars, *refs[:count], *refs[first : first + made], *refs[first + made + 1 + len(through) :])

        results = pl.pallas_call(
            run,
            grid_spec=pltpu.PrefetchScalarGridSpec(
                num_scalar_prefetch=1,
                grid=grid,
                in_specs=[*ins, *[anywhere] * later],
                out_specs=[spec for spec, _ in outs] + [pl.BlockSpec(memory_space=pltpu.SMEM)] + [anywhere] * len(through),
                scratch_shapes=scratch,
            ),
            out_shape=[shape for _, shape in outs]
            + [shaped(self.scalars.shape, jnp.int32)]
            + [shaped(v.shape, v.dtype) for v in through],
            input_output_aliases={1 + count + len(after) + i: made + 1 + i for i in range(len(through))},
            compiler_params=pltpu.CompilerParams(vmem_limit_bytes=vmem * 2**20),
            cost_estimate=pl.CostEstimate(flops=int(work * WORK), bytes_accessed=1, transcendentals=0),
            name=name,
        )(self.scalars, *operands, *after, *through)
        self.scalars = results[made]
        return results[:made] + results[made + 1 :]


SIDE, OTHER_SIDE, LENGTH, FIRST, SECOND, CORE, OTHER_CORE = range(7)


def shaped(shape, dtype):
    return jax.ShapeDtypeStruct(shape, dtype)


def held(shape):
    return pl.BlockSpec(shape, lambda *_: (0,) * len(shape), pipeline_mode=pl.Buffered(1))


def turn(values, gain, cosine, sine):
    scale = lax.rsqrt(jnp.mean(values * values, axis=-1, keepdims=True) + EPS_NORM)
    normed = values * scale * gain
    return normed * cosine + pltpu.roll(normed, HD // 2, 1) * sine


def turn_back(grad, values, gain, cosine, sine):
    scale = lax.rsqrt(jnp.mean(values * values, axis=-1, keepdims=True) + EPS_NORM)
    d_normed = grad * cosine + pltpu.roll(grad * sine, HD // 2, 1)
    hat = values * scale
    d_gain = jnp.sum(d_normed * hat, axis=0, keepdims=True)
    d_hat = d_normed * gain
    inner = jnp.mean(d_hat * hat, axis=-1, keepdims=True)
    return scale * (d_hat - hat * inner), d_gain


def key_spans(block):
    start = block * ROWS
    free = min(start, LEN_MIN // ROWS * ROWS)
    spans = []
    if free:
        spans.append((0, free, False, False))
    if start > free:
        spans.append((free, start, False, True))
    spans.append((start, start + ROWS, True, start + ROWS > LEN_MIN))
    return spans


def raised_scores(query, keys, span, length):
    first, last, causal, ragged = span
    scores = mm(query, keys[first:last], NT) * (HD**-0.5 * LOG2_E)
    raised = jnp.exp2(scores)
    allowed = None
    shape = raised.shape
    if causal:
        place = lax.broadcasted_iota(jnp.int32, shape, 0) % ROWS
        allowed = lax.broadcasted_iota(jnp.int32, shape, 1) <= place
    if ragged:
        live = lax.broadcasted_iota(jnp.int32, shape, 1) + first < length
        allowed = live if allowed is None else allowed & live
    return raised if allowed is None else jnp.where(allowed, raised, 0.0)


def split_heads(qkv_ref, group):
    width = group * HD
    queries = [qkv_ref[:, h * HD : (h + 1) * HD] for h in range(group)]
    return queries, qkv_ref[:, width : width + HD], qkv_ref[:, width + HD : width + 2 * HD]


def attend_kernel(group, place_ref, own_ref, other_ref, weight_ref, cos_ref, sin_ref, gain_ref, qkv_ref, out_ref):
    side, length = place_ref[SIDE], place_ref[LENGTH]
    half = own_ref.shape[0]
    qkv_ref[pl.ds(pl.multiple_of(side * half, half), half), :] = mm(own_ref[...], weight_ref[...])
    qkv_ref[pl.ds(pl.multiple_of((1 - side) * half, half), half), :] = mm(other_ref[...], weight_ref[...])
    cosine, sine = cos_ref[...], sin_ref[...]
    queries, keys, values = split_heads(qkv_ref, group)
    turned = [turn(q, gain_ref[0:1], cosine, sine).astype(BF) for q in queries]
    keys = turn(keys, gain_ref[1:2], cosine, sine).astype(BF)
    values = values.astype(BF)
    for block in range(qkv_ref.shape[0] // ROWS):
        rows = slice(block * ROWS, (block + 1) * ROWS)
        query = jnp.concatenate([t[rows] for t in turned], axis=0)
        total, mixed = 0.0, 0.0
        for span in key_spans(block):
            raised = raised_scores(query, keys, span, length)
            total = total + jnp.sum(raised, axis=-1, keepdims=True)
            mixed = mixed + mm(raised.astype(BF), values[span[0] : span[1]])
        mixed = (mixed / total).astype(BF)
        for h in range(group):
            out_ref[rows, h * HD : (h + 1) * HD] = mixed[h * ROWS : (h + 1) * ROWS]


def attend_back_kernel(
    group,
    place_ref,
    qkv_ref,
    own_ref,
    other_ref,
    cos_ref,
    sin_ref,
    gain_ref,
    out_ref,
    gain_out,
    grad_ref,
    dk_ref,
    dv_ref,
):
    side, length = place_ref[SIDE], place_ref[LENGTH]
    half = own_ref.shape[0]
    grad_ref[pl.ds(pl.multiple_of(side * half, half), half), :] = own_ref[...]
    grad_ref[pl.ds(pl.multiple_of((1 - side) * half, half), half), :] = other_ref[...]
    cosine, sine = cos_ref[...], sin_ref[...]
    queries, raw_keys, values = split_heads(qkv_ref, group)
    turned = [turn(q, gain_ref[0:1], cosine, sine).astype(BF) for q in queries]
    keys = turn(raw_keys, gain_ref[1:2], cosine, sine).astype(BF)
    values = values.astype(BF)
    dk_ref[...] = jnp.zeros_like(dk_ref)
    dv_ref[...] = jnp.zeros_like(dv_ref)
    q_gain = jnp.zeros((1, HD), F32)
    for block in range(qkv_ref.shape[0] // ROWS):
        rows = slice(block * ROWS, (block + 1) * ROWS)
        query = jnp.concatenate([t[rows] for t in turned], axis=0)
        grad = jnp.concatenate([grad_ref[rows, h * HD : (h + 1) * HD] for h in range(group)], axis=0)
        spans = key_spans(block)
        raised = [raised_scores(query, keys, span, length) for span in spans]
        total = sum(jnp.sum(r, axis=-1, keepdims=True) for r in raised)
        fix = 1.0 / total
        chances = [r * fix for r in raised]
        d_chances = [mm(grad, values[s[0] : s[1]], NT) for s in spans]
        inner = sum(jnp.sum(c * d, axis=-1, keepdims=True) for c, d in zip(chances, d_chances, strict=True))
        d_query = 0.0
        for span, chance, d_chance in zip(spans, chances, d_chances, strict=True):
            d_score = (chance * (d_chance - inner) * (HD**-0.5)).astype(BF)
            part = slice(span[0], span[1])
            d_query = d_query + mm(d_score, keys[part])
            dk_ref[part, :] += mm(d_score, query, TN)
            dv_ref[part, :] += mm(chance.astype(BF), grad, TN)
        for h in range(group):
            cols = slice(h * HD, (h + 1) * HD)
            d_raw, d_gain = turn_back(
                d_query[h * ROWS : (h + 1) * ROWS], qkv_ref[rows, cols], gain_ref[0:1], cosine[rows], sine[rows]
            )
            out_ref[rows, cols] = d_raw.astype(BF)
            q_gain = q_gain + d_gain
    width = group * HD
    d_raw, k_gain = turn_back(dk_ref[...], raw_keys, gain_ref[1:2], cosine, sine)
    out_ref[:, width : width + HD] = d_raw.astype(BF)
    out_ref[:, width + HD : width + 2 * HD] = dv_ref[...].astype(BF)

    @pl.when(pl.program_id(0) == 0)
    def _():
        gain_out[...] = jnp.zeros_like(gain_out)

    gain_out[0:1, :] += q_gain
    gain_out[1:2, :] += k_gain


def attend(order, own, other, weights, cosine, sine, gains, heads, group):
    half, width = own.shape
    cap, cols = 2 * half, (group + 2) * HD
    return order.call(
        functools.partial(attend_kernel, group),
        (heads,),
        [
            held((half, width)),
            held((half, width)),
            pl.BlockSpec((width, cols), lambda n, s: (0, n)),
            held((cap, HD)),
            held((cap, HD)),
            held((2, HD)),
        ],
        [
            (pl.BlockSpec((cap, cols), lambda n, s: (0, n)), shaped((cap, heads * cols), F32)),
            (pl.BlockSpec((cap, group * HD), lambda n, s: (0, n)), shaped((cap, heads * group * HD), BF)),
        ],
        (own, other, weights, cosine, sine, gains),
        work=24,
        name="attend",
    )


def attend_back(order, qkv, own, other, cosine, sine, gains, span, group, after=(), through=()):
    half, cap, cols = own.shape[0], 2 * own.shape[0], (group + 2) * HD
    first, heads = span
    rows = pl.BlockSpec((half, group * HD), lambda n, s: (0, n))
    return order.call(
        functools.partial(attend_back_kernel, group),
        (heads,),
        [
            pl.BlockSpec((cap, cols), lambda n, s: (0, first + n)),
            rows,
            rows,
            held((cap, HD)),
            held((cap, HD)),
            held((2, HD)),
        ],
        [
            (pl.BlockSpec((cap, cols), lambda n, s: (0, n)), shaped((cap, heads * cols), BF)),
            (pl.BlockSpec((8, HD), lambda n, s: (0, 0)), shaped((8, HD), F32)),
        ],
        (qkv, own, other, cosine, sine, gains),
        after=after,
        through=through,
        scratch=[pltpu.VMEM((cap, group * HD), BF), pltpu.VMEM((cap, HD), F32), pltpu.VMEM((cap, HD), F32)],
        work=17,
        name="attend_back",
    )


def project_kernel(count, place_ref, *refs):
    for out_ref, at in ((refs[-2], 0), (refs[-1], refs[-2].shape[1])):
        cols = slice(at, at + out_ref.shape[1])
        out_ref[...] = sum(mm(refs[i][...], refs[count + i][:, cols]) for i in range(count)).astype(BF)


def project(order, rows, weights, cols, through=()):
    half, depth = rows.shape[0], weights[0][0].shape[0]
    left = [pl.BlockSpec((half, depth), functools.partial(lambda at, j, s: (0, s[at]), at)) for _, _, at in weights]
    right = [pl.BlockSpec((depth, cols), functools.partial(lambda at, j, s: (0, at), at)) for _, at, _ in weights]
    out = pl.BlockSpec((half, cols // 2), lambda j, s: (0, 0))
    return order.call(
        functools.partial(project_kernel, len(weights)),
        (1,),
        left + right,
        [(out, shaped((half, cols // 2), BF))] * 2,
        (*[rows] * len(weights), *[w for w, _, _ in weights]),
        through=through,
        work=5,
        name="project",
    )


WIDE = 3 * TILE
PAIR = 2 * TILE


def swiglu_kernel(place_ref, second_own, second_other, back_own, back_other, weight_ref, out_ref):
    half = second_own.shape[0]
    for at, second_ref, back_ref in ((0, second_own, back_own), (half, second_other, back_other)):
        rows = slice(at, at + half)
        pair = mm(second_ref[...], weight_ref[:, :PAIR])
        d_hidden = mm(back_ref[...], weight_ref[:, PAIR:])
        gate, up = pair[:, :TILE], pair[:, TILE:]
        sigmoid = 1.0 / (1.0 + jnp.exp(-gate))
        silu = gate * sigmoid
        d_gate = d_hidden * up * (sigmoid * (1.0 + gate * (1.0 - sigmoid)))
        out_ref[rows, :TILE] = d_gate.astype(BF)
        out_ref[rows, TILE:PAIR] = (d_hidden * silu).astype(BF)
        out_ref[rows, PAIR:] = (silu * up).astype(BF)


def swiglu(order, second, back, weights, first_tile, tiles, after=(), through=()):
    half, width = second[0].shape
    rows = held((half, width))
    return order.call(
        swiglu_kernel,
        (tiles,),
        [rows, rows, rows, rows, pl.BlockSpec((width, WIDE), lambda j, s: (0, first_tile + j))],
        [(pl.BlockSpec((2 * half, WIDE), lambda j, s: (0, j)), shaped((2 * half, tiles * WIDE), BF))],
        (*second, *back, weights),
        after=after,
        through=through,
        work=5 * tiles,
        name="swiglu",
    )


def turn_columns_kernel(which, place_ref, own_keep, other_keep, own_send, other_send, keep_ref, send_ref):
    half = own_keep.shape[0]
    if which is None:
        own_at, other_at = slice(0, half), slice(half, 2 * half)
    else:
        own_at = pl.ds(pl.multiple_of(place_ref[which] * half, half), half)
        other_at = pl.ds(pl.multiple_of((1 - place_ref[which]) * half, half), half)
    keep_ref[:, own_at] = own_keep[...].T
    keep_ref[:, other_at] = other_keep[...].T
    send_ref[:, own_at] = own_send[...].T
    send_ref[:, other_at] = other_send[...].T


def turn_columns(order, own, other, which, axes, after=()):
    half = own.shape[0]
    owned = own.shape[1] // 16
    y, c = lax.axis_index(axes[1]), lax.axis_index(axes[2])
    at = lambda j, mine: (j % 4) * 4 + jnp.where(j < 4, 1 - y, y) * 2 + jnp.where(mine, c, 1 - c)
    lines = jnp.arange(8, dtype=jnp.int32)
    table = jnp.concatenate([at(lines, True), at(lines, False)]).astype(jnp.int32)
    scalars = jnp.concatenate([order.scalars, table])
    base = order.scalars.shape[0]
    keep = pl.BlockSpec((half, owned), lambda j, s: (0, s[base + j]))
    send = pl.BlockSpec((half, owned), lambda j, s: (0, s[base + 8 + j]))
    out = pl.BlockSpec((owned, 2 * half), lambda j, s: (j, 0))
    held_back, order.scalars = order.scalars, scalars
    keep_cols, send_cols = order.call(
        functools.partial(turn_columns_kernel, which),
        (8,),
        [keep, keep, send, send],
        [(out, shaped((8 * owned, 2 * half), BF))] * 2,
        (own, other, own, other),
        after=after,
        work=7,
        name="turn_columns",
    )
    order.scalars = order.scalars[:base]
    return keep_cols, send_cols


def weight_grad_kernel(splits, place_ref, *refs):
    lefts, (own_ref, other_ref, *outs) = refs[: 2 * len(splits)], refs[2 * len(splits) :]
    half = lefts[0].shape[0] // 2
    for i, (first, last) in enumerate(splits):
        cols = slice(first, last)
        product = mm(lefts[2 * i][...], own_ref[:, cols]) + mm(lefts[2 * i + 1][...], other_ref[:, cols])
        if len(outs) == 2:
            outs[0][:, cols] = product[:half].astype(BF)
            outs[1][:, cols] = product[half:].astype(BF)
            continue
        for line in range(4):
            at, owned = line * half // 2, half // 4
            outs[0][at : at + owned, cols] = product[line * owned : (line + 1) * owned].astype(BF)
            outs[0][at + owned : at + 2 * owned, cols] = product[half + line * owned : half + (line + 1) * owned].astype(BF)


def weight_grad(order, lefts, splits, own, other, step, by_line=False, after=(), through=()):
    rows, cap = lefts[0][0].shape
    cols = own.shape[1]
    right = pl.BlockSpec((cap, step), lambda j, s: (0, j))
    outs = [(pl.BlockSpec((rows // 2, step), lambda j, s: (0, j)), shaped((rows // 2, cols), BF))] * 2
    if by_line:
        outs = [(pl.BlockSpec((rows, step), lambda j, s: (0, j)), shaped((rows, cols), BF))]
    return order.call(
        functools.partial(weight_grad_kernel, splits),
        (cols // step,),
        [held((rows, cap))] * (2 * len(lefts)) + [right, right],
        outs,
        (*[part for pair in lefts for part in pair], own, other),
        after=after,
        through=through,
        work=cols // 160,
        name="weight_grad",
    )


def contract_kernel(count, ranges, adds, place_ref, *refs):
    outs = refs[2 * count + adds :]
    for out_ref, spans in zip(outs, ranges, strict=True):
        total = 0.0
        for i in range(count):
            for first, last in spans:
                total = total + mm(refs[i][:, first:last], refs[count + i][:, first:last], NT)
        for i in range(adds):
            total = total + refs[2 * count + i][...].astype(F32)
        out_ref[...] = total.astype(out_ref.dtype)


def contract(order, which, lefts, weights, ranges, dtypes, adds=(), after=()):
    half, step = lefts[0].shape[0] // 2, 256
    width = weights[0][0].shape[0]
    ins = [pl.BlockSpec((half, a.shape[1]), lambda j, s: (s[which], 0), pipeline_mode=pl.Buffered(1)) for a in lefts]
    ins += [
        pl.BlockSpec((step, a.shape[1]), functools.partial(lambda block, j, s: (j, block), block))
        for a, (_, block) in zip(lefts, weights, strict=True)
    ]
    across = pl.BlockSpec((half, step), lambda j, s: (0, j))
    ins += [across] * len(adds)
    return order.call(
        functools.partial(contract_kernel, len(lefts), ranges, len(adds)),
        (width // step,),
        ins,
        [(across, shaped((half, width), t)) for t in dtypes],
        (*lefts, *[w for w, _ in weights], *adds),
        after=after,
        work=sum(a.shape[1] for a in lefts) // 400,
        name="contract",
    )


LINES = 128


def lines_spec(width):
    return pl.BlockSpec((LINES, width), lambda j, s: (j, 0))


def middle_kernel(place_ref, tokens_ref, own_ref, sent_ref, gain_ref, middle_ref, second_ref):
    middle = tokens_ref[...].astype(F32) + own_ref[...] + sent_ref[...].astype(F32)
    middle_ref[...] = middle
    second_ref[...] = (middle * rms_parts(middle) * gain_ref[1:2, :]).astype(BF)


def middle_rows(order, tokens, own, sent, gains, after=()):
    rows, width = tokens.shape
    spec = lines_spec(width)
    return order.call(
        middle_kernel,
        (rows // LINES,),
        [spec, spec, spec, held((2, width))],
        [(spec, shaped((rows, width), F32)), (spec, shaped((rows, width), BF))],
        (tokens, own, sent, gains),
        after=after,
        work=6,
        name="middle_rows",
    )


def norm_back_kernel(which, place_ref, own_ref, sent_ref, value_ref, extra_ref, gain_ref, *outs):
    grad = own_ref[...] + sent_ref[...].astype(F32)
    values = value_ref[...].astype(F32)
    scale = rms_parts(values)
    hat = values * scale
    d_hat = grad * gain_ref[which : which + 1, :]
    inner = jnp.mean(d_hat * hat, axis=-1, keepdims=True)
    total = extra_ref[...].astype(F32) + scale * (d_hat - hat * inner)
    outs[0][...] = total
    for out in outs[1:-1]:
        out[...] = total.astype(BF)

    @pl.when(pl.program_id(0) == 0)
    def _():
        outs[-1][...] = jnp.zeros_like(outs[-1])

    outs[-1][0:1, :] += jnp.sum(grad * hat, axis=0, keepdims=True)


def norm_back(order, which, own, sent, values, extra, gains, low):
    rows, width = own.shape
    spec = lines_spec(width)
    outs = [(spec, shaped((rows, width), F32))]
    outs += [(spec, shaped((rows, width), BF))] * low
    outs.append((pl.BlockSpec((8, width), lambda j, s: (0, 0)), shaped((8, width), F32)))
    return order.call(
        functools.partial(norm_back_kernel, which),
        (rows // LINES,),
        [spec, spec, spec, spec, held((2, width))],
        outs,
        (own, sent, values, extra, gains),
        work=8,
        name="norm_back",
    )


def add_kernel(place_ref, *refs):
    at = 0
    for i in range(len(refs) // 2):
        a, b = refs[2 * i], refs[2 * i + 1]
        refs[-1][:, at : at + a.shape[1]] = (a[...].astype(F32) + b[...].astype(F32)).astype(BF)
        at += a.shape[1]


def add_pairs(order, pairs, skip=0):
    rows = pairs[0][1].shape[0]
    lines = min(LINES, rows)
    flat = [part for pair in pairs for part in pair]
    width = sum(a.shape[1] for a, _ in pairs)
    spec = lambda width, skip: pl.BlockSpec((lines, width), lambda j, s: (j + skip, 0))
    return order.call(
        add_kernel,
        (rows // lines,),
        [spec(a.shape[1], skip * (i == 0)) for pair in pairs for i, a in enumerate(pair)],
        [(spec(width, 0), shaped((rows, width), BF))],
        flat,
        work=5,
        name="add_pairs",
    )[0]


def take_kernel(place_ref, from_ref, out_ref):
    out_ref[...] = from_ref[...]


def take_rows(order, array):
    rows, width = array.shape
    block = pl.BlockSpec((rows // 2, width), lambda j, s: (0, 0))
    return order.call(
        take_kernel, (1,), [block], [(block, shaped((rows // 2, width), array.dtype))], [array], work=2, name="take_rows"
    )[0]


def beside_kernel(place_ref, *refs):
    at = 0
    for ref in refs[:-1]:
        refs[-1][:, at : at + ref.shape[1]] = ref[...]
        at += ref.shape[1]


def beside(order, arrays):
    rows, width = arrays[0].shape[0], sum(a.shape[1] for a in arrays)
    whole = [pl.BlockSpec(a.shape, lambda j, s: (0, 0)) for a in arrays]
    out = (pl.BlockSpec((rows, width), lambda j, s: (0, 0)), shaped((rows, width), arrays[0].dtype))
    return order.call(beside_kernel, (1,), whole, [out], arrays, work=2, name="beside")


def adam_kernel(rates, place_ref, *refs):
    pair, down, sums, pair_out, down_out = refs[0:3], refs[3:6], refs[6], refs[7:10], refs[10:13]
    for i in range(2):
        new = adam_step(*[r[:, i, :] for r in pair], sums[:, i * TILE : (i + 1) * TILE].astype(F32), rates[0], WEIGHT_DECAY)
        for out, value in zip(pair_out, new, strict=True):
            out[:, i, :] = value
    new = adam_step(*[r[...] for r in down], sums[:, PAIR:].astype(F32).T, rates[1], WEIGHT_DECAY)
    for out, value in zip(down_out, new, strict=True):
        out[...] = value


def adam_mlp(order, pair, down, sums, rates):
    shard, _, units = pair[0].shape
    wide = pl.BlockSpec((shard, 2, TILE), lambda j, s: (0, 0, j))
    tall = pl.BlockSpec((TILE, shard), lambda j, s: (j, 0))
    return order.call(
        functools.partial(adam_kernel, rates),
        (units // TILE,),
        [wide] * 3 + [tall] * 3 + [pl.BlockSpec((shard, WIDE), lambda j, s: (0, j))],
        [(wide, shaped(pair[0].shape, F32))] * 3 + [(tall, shaped(down[0].shape, F32))] * 3,
        (*pair, *down, sums),
        work=20,
        name="adam_mlp",
    )


def rms_parts(values):
    return lax.rsqrt(jnp.mean(values * values, axis=-1, keepdims=True) + EPS_NORM)


def rope_tables(row_count):
    places = jnp.arange(row_count).astype(F32)
    inverse_freq = ROPE_BASE ** (-(jnp.arange(HD // 2).astype(F32) * 2.0) / HD)
    angles = places[:, None] * inverse_freq[None, :]
    sine = jnp.sin(angles)
    cosine = jnp.cos(angles)
    return jnp.concatenate([cosine, cosine], axis=1), jnp.concatenate([-sine, sine], axis=1)


def adam_step(weight, mean_old, square, gradient, step_rate, decay_rate):
    new_mean = BETA_ONE * mean_old + (1.0 - BETA_ONE) * gradient
    new_square = BETA_TWO * square + (1.0 - BETA_TWO) * gradient * gradient
    fix_one = 1.0 - BETA_ONE**STEP
    fix_two = 1.0 - BETA_TWO**STEP
    update = new_mean / fix_one / (jnp.sqrt(new_square / fix_two) + ADAM_EPS)
    return (weight - step_rate * (update + decay_rate * weight), new_mean, new_square)


class Summer:
    def __init__(self, axes, order, side):
        self.axes, self.order, self.side = axes, order, side
        self.lines = len(axes) == 3

    def other_core(self, piece):
        return lax.ppermute(piece, self.axes[2], [(0, 1), (1, 0)]) if self.lines else None

    def columns(self, own, other, in_order, after=()):
        if not self.lines:
            if not in_order:
                return jnp.concatenate([own, other], axis=0)
            first = self.side == 0
            return jnp.concatenate([jnp.where(first, own, other), jnp.where(first, other, own)], axis=0)
        keep, send = turn_columns(self.order, own, other, SIDE if in_order else None, self.axes, after)
        return keep, self.other_core(send)

    def grad(self, lefts, splits, right, from_core, step, after=(), through=()):
        if not self.lines:
            tiled = right.reshape(right.shape[0], -1, step)
            parts = [
                mm(left, tiled[:, :, first:last].reshape(right.shape[0], -1), TN).reshape(left.shape[1], -1, last - first)
                for left, (first, last) in zip(lefts, splits, strict=True)
            ]
            return jnp.concatenate(parts, axis=2).reshape(lefts[0].shape[1], -1).astype(BF), *through
        near, keep, *handed = weight_grad(self.order, lefts, splits, right, from_core, step, after=after, through=through)
        return keep, lax.ppermute(near, self.axes[1], [(0, 1), (1, 0)]), *handed

    def grad_by_line(self, lefts, splits, right, from_core, step, after=(), through=()):
        if not self.lines:
            first, *handed = self.grad(lefts, splits, right, from_core, step, after, through)
            return self.finish((first,)), *handed
        whole, *handed = weight_grad(self.order, lefts, splits, right, from_core, step, True, after, through)
        return lax.psum_scatter(whole, self.axes[0], scatter_dimension=0, tiled=True), *handed

    def trade_by_line(self, summed):
        if not self.lines:
            return None
        return lax.ppermute(take_rows(self.order, summed), self.axes[1], [(0, 1), (1, 0)])

    def finish_by_line(self, summed, got):
        return add_pairs(self.order, [(summed, got)], 1) if self.lines else summed

    def finish(self, *grads):
        if not self.lines:
            return lax.psum_scatter(jnp.concatenate([g for g, in grads], axis=1), self.axes, scatter_dimension=0, tiled=True)
        line = add_pairs(self.order, grads)
        return lax.psum_scatter(line, self.axes[0], scatter_dimension=0, tiled=True)

    def everywhere(self, values):
        if not self.lines:
            return lax.psum(values, (*self.axes, "tensor"))
        pair = [(0, 1), (1, 0)]
        steps = [(self.axes[2], pair), ("tensor", pair), (self.axes[1], pair)]
        steps += [(self.axes[0], [(0, 1), (1, 0), (2, 3), (3, 2)]), (self.axes[0], [(0, 2), (2, 0), (1, 3), (3, 1)])]
        for axis, pairs in steps:
            values = values + lax.ppermute(values, axis, pairs)
        return values


def on_device(
    axes,
    tokens,
    cotangent,
    lengths,
    w_query,
    query_mean,
    query_square,
    w_keyval,
    keyval_mean,
    keyval_square,
    w_out,
    out_mean,
    out_square,
    w_gateup,
    gateup_mean,
    gateup_square,
    w_down,
    down_mean,
    down_square,
    norm_gains,
    norm_mean,
    norm_square,
    head_gains,
    head_mean,
    head_square,
):
    side = lax.axis_index("tensor")
    tok_rows = tokens.shape[0]
    cap = 2 * tok_rows
    length = lengths[0]
    order = Order(side, length, lax.axis_index(axes[2]) if len(axes) == 3 else jnp.zeros_like(side))
    summer = Summer(axes, order, side)

    def swap(piece):
        return lax.ppermute(piece, "tensor", [(0, 1), (1, 0)])

    def there(*arrays):
        return [v for v in arrays if v is not None]

    def gather(shard):
        return lax.all_gather(shard, axes, axis=0, tiled=True)

    shard = w_query.shape[0]
    heads = w_keyval.shape[2] // HD
    group = w_query.shape[1] // HD // heads
    units = w_gateup.shape[2]
    tiles = units // TILE
    part = tiles // CHUNKS
    kv_low = w_keyval.astype(BF).reshape(shard, 2, heads, HD)
    qkv_shard = jnp.concatenate(
        [w_query.astype(BF).reshape(shard, heads, group * HD), kv_low[:, 0], kv_low[:, 1]], axis=2
    ).reshape(shard, heads * (group + 2) * HD)
    out_shard = w_out.astype(BF).T
    pair_low = w_gateup.astype(BF).reshape(shard, 2, tiles, TILE)
    down_low = w_down.astype(BF).T.reshape(shard, tiles, TILE)
    mlp_shard = jnp.concatenate([pair_low[:, 0], pair_low[:, 1], down_low], axis=2).reshape(shard, tiles * WIDE)

    stream = tokens.astype(F32)
    normed_own = (stream * rms_parts(stream) * norm_gains[0]).astype(BF)
    normed_other = swap(normed_own)
    qkv_cols, out_cols = qkv_shard.shape[1], out_shard.shape[1]
    early = gather(jnp.concatenate([qkv_shard, out_shard], axis=1))
    most = gather(mlp_shard[:, : (CHUNKS - 1) * part * WIDE])
    late = gather(mlp_shard[:, (CHUNKS - 1) * part * WIDE :])
    parts = [(most, part * p) for p in range(CHUNKS - 1)] + [(late, 0)]

    own_places = side * tok_rows + jnp.arange(tok_rows)
    live = (own_places < length)[:, None]
    back_own = jnp.where(live, cotangent, jnp.zeros_like(cotangent))
    back_other = swap(back_own)
    cosine, sine = rope_tables(cap)

    def there(*arrays):
        return [v for v in arrays if v is not None]

    normed_cols = summer.columns(normed_own, normed_other, True)

    qkv, attended = attend(order, normed_own, normed_other, early, cosine, sine, head_gains, heads, group)
    attended_core = summer.other_core(attended)
    out_block = [(early, qkv_cols // out_cols)]
    whole_out = [[(0, out_cols)]]
    attended_sent = swap(contract(order, OTHER_SIDE, [attended], out_block, whole_out, [BF])[0])
    back_cols = summer.columns(back_own, back_other, False)
    (attended_here,) = contract(
        order, SIDE, [attended], out_block, whole_out, [F32], after=there(normed_cols[1], attended_core)
    )
    middle, second_own = middle_rows(order, tokens, attended_here, attended_sent, norm_gains)

    second = (second_own, swap(second_own))
    back = (back_own, back_other)
    pair_spans = [(t * WIDE, t * WIDE + PAIR) for t in range(part)]
    down_spans = [(t * WIDE + PAIR, (t + 1) * WIDE) for t in range(part)]
    blocks = [(w, at // part) for w, at in parts]

    def mlp(p, after=(), through=()):
        piece, *handed = swiglu(order, second, back, parts[p][0], parts[p][1], part, after, through)
        return (piece, summer.other_core(piece)), *handed

    def mlp_grad(p, after=(), through=()):
        return summer.grad([second_cols, back_cols], [(0, PAIR), (PAIR, WIDE)], *mlp_pieces[p], WIDE, after, through)

    out_rows = early.shape[0] // 2
    core = order.scalars[CORE]
    out_half = lax.dynamic_slice(early, (core * out_rows, qkv_cols), (out_rows, out_cols))

    second_cols = summer.columns(*second, False)
    mlp_pieces = [*mlp(0, there(back_cols[1])), *mlp(1)]
    splits = [(0, PAIR), (PAIR, WIDE)]
    first_sum, out_half = summer.grad_by_line([second_cols, back_cols], splits, *mlp_pieces[0], WIDE, through=[out_half])
    out_got = swap(out_half)
    pieces = [piece for piece, _ in mlp_pieces]
    (d_second_part,) = contract(order, SECOND, pieces, blocks[:2], [pair_spans], [BF])
    mlp_grads = [mlp_grad(1)]
    mlp_pieces += mlp(2, [out_got])
    pieces = [piece for piece, _ in mlp_pieces]
    d_second_sent = swap(contract(order, SECOND, pieces[2:], blocks[2:], [pair_spans], [BF], [d_second_part])[0])
    if summer.lines:
        out_other = [(out_got, 0, CORE), (summer.other_core(out_got), 0, OTHER_CORE)]
    else:
        out_other = [(swap(early[:, qkv_cols:]), 0, FIRST)]
    mlp_grads.append(mlp_grad(2))
    (d_second,) = contract(order, FIRST, pieces, blocks, [pair_spans], [F32])
    d_middle, branch_own, branch_again, g_second_gain = norm_back(
        order, 1, d_second, d_second_sent, middle, back_own, norm_gains, 2
    )

    there_a, there_b = project(order, branch_own, out_other, out_cols)
    sent_a, sent_b = swap(there_a), swap(there_b)
    mlp_sums = [summer.finish(mlp_grads[0])]
    here_a, here_b, branch_again = project(
        order, branch_own, [(early, qkv_cols // out_cols, FIRST)], out_cols, [branch_again]
    )
    branch_other = swap(branch_again)

    def attention_back(half, here, sent, after=(), through=()):
        span = (half * heads // 2, heads // 2)
        d_part, g_part, *handed = attend_back(
            order, qkv, here, sent, cosine, sine, head_gains, span, group, after, through
        )
        return d_part, summer.other_core(d_part), g_part[:2], *handed

    d_qkv_a, core_a, g_head_a = attention_back(0, here_a, sent_a)
    d_qkv_b, core_b, g_head_b = attention_back(1, here_b, sent_b)
    (out_there,) = contract(order, SECOND, pieces, blocks, [down_spans], [BF])
    out_sent = swap(out_there)
    branch_cols = summer.columns(branch_again, branch_other, True)
    mlp_sums.append(summer.finish(mlp_grads[1]))
    first_got = summer.trade_by_line(first_sum)
    qkv_grad_a = summer.grad([normed_cols], [(0, 512)], d_qkv_a, core_a, 512)
    qkv_grad_b = summer.grad([normed_cols], [(0, 512)], d_qkv_b, core_b, 512)
    out_grad = summer.grad([branch_cols], [(0, 512)], attended, attended_core, 512)
    d_qkv = [d_qkv_a, d_qkv_b]
    qkv_blocks = [(early, 0), (early, 1)]
    whole_qkv = [[(0, qkv_cols // 2)]]
    d_first_sent = swap(contract(order, OTHER_SIDE, d_qkv, qkv_blocks, whole_qkv, [BF])[0])
    qkv_sum_a = summer.finish(qkv_grad_a)
    (d_first,) = contract(order, SIDE, d_qkv, qkv_blocks, whole_qkv, [F32], after=mlp_sums[:1])
    (layer_out,) = contract(order, FIRST, pieces, blocks, [down_spans], [F32], [middle, out_sent])
    last_sum = summer.finish(qkv_grad_b, out_grad)
    mlp_sums.insert(0, summer.finish_by_line(first_sum, first_got))
    tokens_grad, g_first_gain = norm_back(order, 0, d_first, d_first_sent, tokens, d_middle, norm_gains, 0)
    wide_rate = RATE_SCALE * D ** (-0.5)
    mlp_new = adam_mlp(
        order,
        (w_gateup, gateup_mean, gateup_square),
        (w_down, down_mean, down_square),
        jnp.concatenate(mlp_sums, axis=1),
        (wide_rate, RATE_SCALE * FF ** (-0.5)),
    )
    (qkv_sum,) = beside(order, [qkv_sum_a, last_sum[:, : qkv_cols // 2]])
    out_sum = last_sum[:, qkv_cols // 2 :]
    g_head = g_head_a + g_head_b

    out_sum = out_sum.astype(F32).T
    qkv_sum = qkv_sum.astype(F32).reshape(shard, heads, (group + 2) * HD)
    query_sum = qkv_sum[:, :, : group * HD].reshape(shard, heads * group * HD)
    keyval_sum = jnp.stack(
        [
            qkv_sum[:, :, group * HD : (group + 1) * HD].reshape(shard, heads * HD),
            qkv_sum[:, :, (group + 1) * HD :].reshape(shard, heads * HD),
        ],
        axis=1,
    )
    gains_here = jnp.concatenate([g_first_gain[0], g_second_gain[0], g_head.reshape(-1)]).reshape(-1, HD)
    gain_sums = summer.everywhere(gains_here).reshape(-1)
    norm_sum = gain_sums[: 2 * D].reshape(2, D)
    head_sum = gain_sums[2 * D :].reshape(2, HD)

    query_new = adam_step(w_query, query_mean, query_square, query_sum, wide_rate, WEIGHT_DECAY)
    keyval_new = adam_step(w_keyval, keyval_mean, keyval_square, keyval_sum, wide_rate, WEIGHT_DECAY)
    out_new = adam_step(w_out, out_mean, out_square, out_sum, RATE_SCALE * OUT_FAN ** (-0.5), WEIGHT_DECAY)
    norm_new = adam_step(norm_gains, norm_mean, norm_square, norm_sum, GAIN_RATE, 0.0)
    head_new = adam_step(head_gains, head_mean, head_square, head_sum, GAIN_RATE, 0.0)
    return (layer_out, tokens_grad, *query_new, *keyval_new, *out_new, *mlp_new, *norm_new, *head_new)


def solution(mesh):
    count, sides = mesh.shape["dp"], mesh.shape["tensor"]
    if count == 16:
        axes = ("z", "y", "core")
        grid = Mesh(mesh.devices.reshape(4, 2, 2, sides), (*axes, "tensor"))
    else:
        axes, grid = ("dp",), mesh
    rows = P((*axes, "tensor"), None)
    in_out = [P(axes, "tensor")] * 3 + [P(axes, None, "tensor")] * 3 + [P("tensor", axes)] * 3
    in_out += [P(axes, None, "tensor")] * 3 + [P("tensor", axes)] * 3 + [P()] * 6
    return jax.shard_map(
        functools.partial(on_device, axes),
        mesh=grid,
        in_specs=(rows, rows, P(axes), *in_out),
        out_specs=(rows, rows, *in_out),
        check_vma=False,
    )
```

```python
import functools

import jax
import jax.numpy as jnp
from jax import lax
from jax.experimental import pallas as pl
from jax.experimental.pallas import tpu as pltpu
from jax.sharding import Mesh
from jax.sharding import PartitionSpec as P

D = 2048
HD = 128
FF = 6144
STEP = 10
LEN_MIN = 640

EPS_NORM = 1e-06
ROPE_BASE = 1000000.0
BETA_ONE = 0.9
BETA_TWO = 0.95
ADAM_EPS = 1e-08
WEIGHT_DECAY = 0.1
RATE_SCALE = 2.0
GAIN_RATE = 0.6
OUT_FAN = 8.0
LOG2_E = 1.4426950408889634

BF = jnp.bfloat16
F32 = jnp.float32
ROWS = 256
TILE = 256
BLOCK = 1024
CHUNKS = 3
WORK = 10**10

NN = (((1,), (0,)), ((), ()))
NT = (((1,), (1,)), ((), ()))
TN = (((0,), (0,)), ((), ()))


def mm(a, b, dims=NN):
    return lax.dot_general(a, b, dims, preferred_element_type=F32)


class Order:
    def __init__(self, side, length, core):
        self.rate = WORK
        one = jnp.ones_like(side)
        self.scalars = jnp.stack([side, 1 - side, length, 0 * one, one, core, 1 - core]).astype(jnp.int32)

    def call(self, kernel, grid, ins, outs, operands, *, after=(), through=(), vmem=48, scratch=(), work, name):
        count, later, made = len(ins), len(after) + len(through), len(outs)
        anywhere = pl.BlockSpec(memory_space=pl.ANY)

        def run(scalars, *refs):
            first = count + later
            token = refs[first + made]
            for i in range(token.shape[0]):
                token[i] = scalars[i]
            kernel(scalars, *refs[:count], *refs[first : first + made], *refs[first + made + 1 + len(through) :])

        results = pl.pallas_call(
            run,
            grid_spec=pltpu.PrefetchScalarGridSpec(
                num_scalar_prefetch=1,
                grid=grid,
                in_specs=[*ins, *[anywhere] * later],
                out_specs=[spec for spec, _ in outs] + [pl.BlockSpec(memory_space=pltpu.SMEM)] + [anywhere] * len(through),
                scratch_shapes=scratch,
            ),
            out_shape=[shape for _, shape in outs]
            + [shaped(self.scalars.shape, jnp.int32)]
            + [shaped(v.shape, v.dtype) for v in through],
            input_output_aliases={1 + count + len(after) + i: made + 1 + i for i in range(len(through))},
            compiler_params=pltpu.CompilerParams(vmem_limit_bytes=vmem * 2**20),
            cost_estimate=pl.CostEstimate(flops=int(work * self.rate) + 1, bytes_accessed=1, transcendentals=0),
            name=name,
        )(self.scalars, *operands, *after, *through)
        self.scalars = results[made]
        return results[:made] + results[made + 1 :]


SIDE, OTHER_SIDE, LENGTH, FIRST, SECOND, CORE, OTHER_CORE = range(7)


def shaped(shape, dtype):
    return jax.ShapeDtypeStruct(shape, dtype)


def held(shape):
    return pl.BlockSpec(shape, lambda *_: (0,) * len(shape), pipeline_mode=pl.Buffered(1))


def turn(values, gain, cosine, sine):
    scale = lax.rsqrt(jnp.mean(values * values, axis=-1, keepdims=True) + EPS_NORM)
    normed = values * scale * gain
    return normed * cosine + pltpu.roll(normed, HD // 2, 1) * sine


def turn_back(grad, values, gain, cosine, sine):
    scale = lax.rsqrt(jnp.mean(values * values, axis=-1, keepdims=True) + EPS_NORM)
    d_normed = grad * cosine + pltpu.roll(grad * sine, HD // 2, 1)
    hat = values * scale
    d_gain = jnp.sum(d_normed * hat, axis=0, keepdims=True)
    d_hat = d_normed * gain
    inner = jnp.mean(d_hat * hat, axis=-1, keepdims=True)
    return scale * (d_hat - hat * inner), d_gain


def key_spans(block):
    start = block * ROWS
    free = min(start, LEN_MIN // ROWS * ROWS)
    spans = []
    if free:
        spans.append((0, free, False, False))
    if start > free:
        spans.append((free, start, False, True))
    spans.append((start, start + ROWS, True, start + ROWS > LEN_MIN))
    return spans


def raised_scores(query, keys, span, length):
    first, last, causal, ragged = span
    scores = mm(query, keys[first:last], NT) * (HD**-0.5 * LOG2_E)
    raised = jnp.exp2(scores)
    allowed = None
    shape = raised.shape
    if causal:
        place = lax.broadcasted_iota(jnp.int32, shape, 0) % ROWS
        allowed = lax.broadcasted_iota(jnp.int32, shape, 1) <= place
    if ragged:
        live = lax.broadcasted_iota(jnp.int32, shape, 1) + first < length
        allowed = live if allowed is None else allowed & live
    return raised if allowed is None else jnp.where(allowed, raised, 0.0)


def split_heads(qkv_ref, group):
    width = group * HD
    queries = [qkv_ref[:, h * HD : (h + 1) * HD] for h in range(group)]
    return queries, qkv_ref[:, width : width + HD], qkv_ref[:, width + HD : width + 2 * HD]


def attend_kernel(group, place_ref, own_ref, other_ref, weight_ref, cos_ref, sin_ref, gain_ref, qkv_ref, out_ref):
    side, length = place_ref[SIDE], place_ref[LENGTH]
    half = own_ref.shape[0]
    qkv_ref[pl.ds(pl.multiple_of(side * half, half), half), :] = mm(own_ref[...], weight_ref[...])
    qkv_ref[pl.ds(pl.multiple_of((1 - side) * half, half), half), :] = mm(other_ref[...], weight_ref[...])
    cosine, sine = cos_ref[...], sin_ref[...]
    queries, keys, values = split_heads(qkv_ref, group)
    turned = [turn(q, gain_ref[0:1], cosine, sine).astype(BF) for q in queries]
    keys = turn(keys, gain_ref[1:2], cosine, sine).astype(BF)
    values = values.astype(BF)
    for block in range(qkv_ref.shape[0] // ROWS):
        rows = slice(block * ROWS, (block + 1) * ROWS)
        query = jnp.concatenate([t[rows] for t in turned], axis=0)
        total, mixed = 0.0, 0.0
        for span in key_spans(block):
            raised = raised_scores(query, keys, span, length)
            total = total + jnp.sum(raised, axis=-1, keepdims=True)
            mixed = mixed + mm(raised.astype(BF), values[span[0] : span[1]])
        mixed = (mixed / total).astype(BF)
        for h in range(group):
            out_ref[rows, h * HD : (h + 1) * HD] = mixed[h * ROWS : (h + 1) * ROWS]


def attend_back_kernel(
    group,
    place_ref,
    qkv_ref,
    own_ref,
    other_ref,
    cos_ref,
    sin_ref,
    gain_ref,
    out_ref,
    gain_out,
    grad_ref,
    dk_ref,
    dv_ref,
):
    side, length = place_ref[SIDE], place_ref[LENGTH]
    half = own_ref.shape[0]
    grad_ref[pl.ds(pl.multiple_of(side * half, half), half), :] = own_ref[...]
    grad_ref[pl.ds(pl.multiple_of((1 - side) * half, half), half), :] = other_ref[...]
    cosine, sine = cos_ref[...], sin_ref[...]
    queries, raw_keys, values = split_heads(qkv_ref, group)
    turned = [turn(q, gain_ref[0:1], cosine, sine).astype(BF) for q in queries]
    keys = turn(raw_keys, gain_ref[1:2], cosine, sine).astype(BF)
    values = values.astype(BF)
    dk_ref[...] = jnp.zeros_like(dk_ref)
    dv_ref[...] = jnp.zeros_like(dv_ref)
    q_gain = jnp.zeros((1, HD), F32)
    for block in range(qkv_ref.shape[0] // ROWS):
        rows = slice(block * ROWS, (block + 1) * ROWS)
        query = jnp.concatenate([t[rows] for t in turned], axis=0)
        grad = jnp.concatenate([grad_ref[rows, h * HD : (h + 1) * HD] for h in range(group)], axis=0)
        spans = key_spans(block)
        raised = [raised_scores(query, keys, span, length) for span in spans]
        total = sum(jnp.sum(r, axis=-1, keepdims=True) for r in raised)
        fix = 1.0 / total
        chances = [r * fix for r in raised]
        d_chances = [mm(grad, values[s[0] : s[1]], NT) for s in spans]
        inner = sum(jnp.sum(c * d, axis=-1, keepdims=True) for c, d in zip(chances, d_chances, strict=True))
        d_query = 0.0
        for span, chance, d_chance in zip(spans, chances, d_chances, strict=True):
            d_score = (chance * (d_chance - inner) * (HD**-0.5)).astype(BF)
            part = slice(span[0], span[1])
            d_query = d_query + mm(d_score, keys[part])
            dk_ref[part, :] += mm(d_score, query, TN)
            dv_ref[part, :] += mm(chance.astype(BF), grad, TN)
        for h in range(group):
            cols = slice(h * HD, (h + 1) * HD)
            d_raw, d_gain = turn_back(
                d_query[h * ROWS : (h + 1) * ROWS], qkv_ref[rows, cols], gain_ref[0:1], cosine[rows], sine[rows]
            )
            out_ref[rows, cols] = d_raw.astype(BF)
            q_gain = q_gain + d_gain
    width = group * HD
    d_raw, k_gain = turn_back(dk_ref[...], raw_keys, gain_ref[1:2], cosine, sine)
    out_ref[:, width : width + HD] = d_raw.astype(BF)
    out_ref[:, width + HD : width + 2 * HD] = dv_ref[...].astype(BF)

    @pl.when(pl.program_id(0) == 0)
    def _():
        gain_out[...] = jnp.zeros_like(gain_out)

    gain_out[0:1, :] += q_gain
    gain_out[1:2, :] += k_gain


def attend(order, own, other, weights, cosine, sine, gains, heads, group):
    half, width = own.shape
    cap, cols = 2 * half, (group + 2) * HD
    return order.call(
        functools.partial(attend_kernel, group),
        (heads,),
        [
            held((half, width)),
            held((half, width)),
            pl.BlockSpec((width, cols), lambda n, s: (0, n)),
            held((cap, HD)),
            held((cap, HD)),
            held((2, HD)),
        ],
        [
            (pl.BlockSpec((cap, cols), lambda n, s: (0, n)), shaped((cap, heads * cols), F32)),
            (pl.BlockSpec((cap, group * HD), lambda n, s: (0, n)), shaped((cap, heads * group * HD), BF)),
        ],
        (own, other, weights, cosine, sine, gains),
        work=24,
        name="attend",
    )


def attend_back(order, qkv, own, other, cosine, sine, gains, span, group, after=(), through=()):
    half, cap, cols = own.shape[0], 2 * own.shape[0], (group + 2) * HD
    first, heads = span
    rows = pl.BlockSpec((half, group * HD), lambda n, s: (0, n))
    return order.call(
        functools.partial(attend_back_kernel, group),
        (heads,),
        [
            pl.BlockSpec((cap, cols), lambda n, s: (0, first + n)),
            rows,
            rows,
            held((cap, HD)),
            held((cap, HD)),
            held((2, HD)),
        ],
        [
            (pl.BlockSpec((cap, cols), lambda n, s: (0, n)), shaped((cap, heads * cols), BF)),
            (pl.BlockSpec((8, HD), lambda n, s: (0, 0)), shaped((8, HD), F32)),
        ],
        (qkv, own, other, cosine, sine, gains),
        after=after,
        through=through,
        scratch=[pltpu.VMEM((cap, group * HD), BF), pltpu.VMEM((cap, HD), F32), pltpu.VMEM((cap, HD), F32)],
        work=17,
        name="attend_back",
    )


def project_kernel(count, place_ref, *refs):
    for out_ref, at in ((refs[-2], 0), (refs[-1], refs[-2].shape[1])):
        cols = slice(at, at + out_ref.shape[1])
        out_ref[...] = sum(mm(refs[i][...], refs[count + i][:, cols]) for i in range(count)).astype(BF)


def project(order, rows, weights, cols, through=()):
    half, depth = rows.shape[0], weights[0][0].shape[0]
    left = [pl.BlockSpec((half, depth), functools.partial(lambda at, j, s: (0, s[at]), at)) for _, _, at in weights]
    right = [pl.BlockSpec((depth, cols), functools.partial(lambda at, j, s: (0, at), at)) for _, at, _ in weights]
    out = pl.BlockSpec((half, cols // 2), lambda j, s: (0, 0))
    return order.call(
        functools.partial(project_kernel, len(weights)),
        (1,),
        left + right,
        [(out, shaped((half, cols // 2), BF))] * 2,
        (*[rows] * len(weights), *[w for w, _, _ in weights]),
        through=through,
        work=5,
        name="project",
    )


WIDE = 3 * TILE
PAIR = 2 * TILE


def swiglu_kernel(place_ref, second_own, second_other, back_own, back_other, pair_ref, down_ref, grad_ref, hidden_ref):
    half = second_own.shape[0]
    for at, second_ref, back_ref in ((0, second_own, back_own), (half, second_other, back_other)):
        rows = slice(at, at + half)
        pair = mm(second_ref[...], pair_ref[...])
        d_hidden = mm(back_ref[...], down_ref[...])
        gate, up = pair[:, :TILE], pair[:, TILE:]
        sigmoid = 1.0 / (1.0 + jnp.exp(-gate))
        silu = gate * sigmoid
        d_gate = d_hidden * up * (sigmoid * (1.0 + gate * (1.0 - sigmoid)))
        grad_ref[rows, :TILE] = d_gate.astype(BF)
        grad_ref[rows, TILE:] = (d_hidden * silu).astype(BF)
        hidden_ref[rows, :] = (silu * up).astype(BF)


def swiglu(order, second, back, weights, count, tiles, after=(), through=()):
    half, width = second[0].shape
    rows = held((half, width))
    pair_at = lambda j: j // tiles * (3 * tiles // 2) + j % tiles
    down_at = lambda j: j // tiles * (3 * tiles) + 2 * tiles + j % tiles
    return order.call(
        swiglu_kernel,
        (count * tiles,),
        [
            rows,
            rows,
            rows,
            rows,
            pl.BlockSpec((width, PAIR), lambda j, s: (0, pair_at(j))),
            pl.BlockSpec((width, TILE), lambda j, s: (0, down_at(j))),
        ],
        [
            (pl.BlockSpec((2 * half, PAIR), lambda j, s: (0, j)), shaped((2 * half, count * tiles * PAIR), BF)),
            (pl.BlockSpec((2 * half, TILE), lambda j, s: (0, j)), shaped((2 * half, count * tiles * TILE), BF)),
        ],
        (*second, *back, weights, weights),
        after=after,
        through=through,
        work=5 * count * tiles,
        name="swiglu",
    )


def turn_columns_kernel(which, place_ref, own_keep, other_keep, own_send, other_send, keep_ref, send_ref):
    half = own_keep.shape[0]
    if which is None:
        own_at, other_at = slice(0, half), slice(half, 2 * half)
    else:
        own_at = pl.ds(pl.multiple_of(place_ref[which] * half, half), half)
        other_at = pl.ds(pl.multiple_of((1 - place_ref[which]) * half, half), half)
    keep_ref[:, own_at] = own_keep[...].T
    keep_ref[:, other_at] = other_keep[...].T
    send_ref[:, own_at] = own_send[...].T
    send_ref[:, other_at] = other_send[...].T


def turn_columns(order, own, other, which, axes, after=()):
    half = own.shape[0]
    owned = own.shape[1] // 16
    y, c = lax.axis_index(axes[1]), lax.axis_index(axes[2])
    at = lambda j, mine: (j % 4) * 4 + jnp.where(j < 4, 1 - y, y) * 2 + jnp.where(mine, c, 1 - c)
    lines = jnp.arange(8, dtype=jnp.int32)
    table = jnp.concatenate([at(lines, True), at(lines, False)]).astype(jnp.int32)
    scalars = jnp.concatenate([order.scalars, table])
    base = order.scalars.shape[0]
    keep = pl.BlockSpec((half, owned), lambda j, s: (0, s[base + j]))
    send = pl.BlockSpec((half, owned), lambda j, s: (0, s[base + 8 + j]))
    out = pl.BlockSpec((owned, 2 * half), lambda j, s: (j, 0))
    held_back, order.scalars = order.scalars, scalars
    keep_cols, send_cols = order.call(
        functools.partial(turn_columns_kernel, which),
        (8,),
        [keep, keep, send, send],
        [(out, shaped((8 * owned, 2 * half), BF))] * 2,
        (own, other, own, other),
        after=after,
        work=7,
        name="turn_columns",
    )
    order.scalars = order.scalars[:base]
    return keep_cols, send_cols


def weight_grad_kernel(widths, place_ref, *refs):
    outs = refs[4 * len(widths) :]
    half = refs[0].shape[0] // 2
    first = 0
    for i, width in enumerate(widths):
        left, far_left, right, far_right = refs[4 * i : 4 * i + 4]
        cols = slice(first, first + width)
        first += width
        product = mm(left[...], right[...]) + mm(far_left[...], far_right[...])
        if len(outs) == 2:
            outs[0][:, cols] = product[:half].astype(BF)
            outs[1][:, cols] = product[half:].astype(BF)
            continue
        for line in range(4):
            at, owned = line * half // 2, half // 4
            outs[0][at : at + owned, cols] = product[line * owned : (line + 1) * owned].astype(BF)
            outs[0][at + owned : at + 2 * owned, cols] = product[half + line * owned : half + (line + 1) * owned].astype(BF)


def weight_grad(order, items, by_line=False, after=()):
    rows, cap = items[0][0][0].shape
    widths = [width for _, _, width, _, _ in items]
    steps, step = items[0][4], sum(widths)
    out_rows = rows if by_line else rows // 2
    out = (pl.BlockSpec((out_rows, step), lambda j, s: (0, j)), shaped((out_rows, steps * step), BF))
    ins = []
    for _, _, width, first, _ in items:
        ins += [held((rows, cap))] * 2
        ins += [pl.BlockSpec((cap, width), functools.partial(lambda first, j, s: (0, first + j), first))] * 2
    return order.call(
        functools.partial(weight_grad_kernel, widths),
        (steps,),
        ins,
        [out] if by_line else [out, out],
        [part for left, right, *_ in items for part in (*left, *right)],
        after=after,
        work=steps * step // 160,
        name="weight_grad",
    )


def contract_kernel(count, adds, place_ref, *refs):
    total = 0.0
    for i in range(count):
        total = total + mm(refs[i][...], refs[count + i][...], NT)
    for i in range(adds):
        total = total + refs[2 * count + i][...].astype(F32)
    refs[-1][...] = total.astype(refs[-1].dtype)


def contract(order, which, pairs, dtype, adds=(), after=()):
    half, width = pairs[0][0].shape[0] // 2, pairs[0][2].shape[0]
    step = 512
    ins = [
        pl.BlockSpec((half, BLOCK), functools.partial(lambda at, j, s: (s[which], at), at), pipeline_mode=pl.Buffered(1))
        for _, at, _, _ in pairs
    ]
    ins += [pl.BlockSpec((step, BLOCK), functools.partial(lambda at, j, s: (j, at), at)) for _, _, _, at in pairs]
    across = pl.BlockSpec((half, step), lambda j, s: (0, j))
    return order.call(
        functools.partial(contract_kernel, len(pairs), len(adds)),
        (width // step,),
        ins + [across] * len(adds),
        [(across, shaped((half, width), dtype))],
        (*[left for left, _, _, _ in pairs], *[weights for _, _, weights, _ in pairs], *adds),
        after=after,
        work=8 * len(pairs),
        name="contract",
    )[0]


def contract_both_kernel(which, count, place_ref, *refs):
    total = 0.0
    for i in range(count):
        total = total + mm(refs[i][...], refs[count + i][...], NT)
    half = total.shape[0] // 2
    first, second = total[:half], total[half:]
    here_ref, there_ref = refs[-2:]
    if which == FIRST:
        here_ref[...], there_ref[...] = first, second.astype(BF)
        return
    here = place_ref[which] == 0
    here_ref[...] = jnp.where(here, first, second)
    there_ref[...] = jnp.where(here, second, first).astype(BF)


def contract_both(order, which, pairs):
    rows, width = pairs[0][0].shape[0], pairs[0][2].shape[0]
    step = 512
    ins = [
        pl.BlockSpec((rows, BLOCK), functools.partial(lambda at, j, s: (0, at), at), pipeline_mode=pl.Buffered(1))
        for _, at, _, _ in pairs
    ]
    ins += [pl.BlockSpec((step, BLOCK), functools.partial(lambda at, j, s: (j, at), at)) for _, _, _, at in pairs]
    across = pl.BlockSpec((rows // 2, step), lambda j, s: (0, j))
    return order.call(
        functools.partial(contract_both_kernel, which, len(pairs)),
        (width // step,),
        ins,
        [(across, shaped((rows // 2, width), F32)), (across, shaped((rows // 2, width), BF))],
        (*[left for left, _, _, _ in pairs], *[weights for _, _, weights, _ in pairs]),
        work=5 * len(pairs),
        name="contract_both",
    )


LINES = 128


def lines_spec(width):
    return pl.BlockSpec((LINES, width), lambda j, s: (j, 0))


def middle_kernel(place_ref, tokens_ref, own_ref, sent_ref, gain_ref, middle_ref, second_ref):
    middle = tokens_ref[...].astype(F32) + own_ref[...] + sent_ref[...].astype(F32)
    middle_ref[...] = middle
    second_ref[...] = (middle * rms_parts(middle) * gain_ref[1:2, :]).astype(BF)


def middle_rows(order, tokens, own, sent, gains, after=()):
    rows, width = tokens.shape
    spec = lines_spec(width)
    return order.call(
        middle_kernel,
        (rows // LINES,),
        [spec, spec, spec, held((2, width))],
        [(spec, shaped((rows, width), F32)), (spec, shaped((rows, width), BF))],
        (tokens, own, sent, gains),
        after=after,
        work=6,
        name="middle_rows",
    )


def norm_back_kernel(which, place_ref, own_ref, sent_ref, value_ref, extra_ref, gain_ref, *outs):
    grad = own_ref[...] + sent_ref[...].astype(F32)
    values = value_ref[...].astype(F32)
    scale = rms_parts(values)
    hat = values * scale
    d_hat = grad * gain_ref[which : which + 1, :]
    inner = jnp.mean(d_hat * hat, axis=-1, keepdims=True)
    total = extra_ref[...].astype(F32) + scale * (d_hat - hat * inner)
    outs[0][...] = total
    for out in outs[1:-1]:
        out[...] = total.astype(BF)

    @pl.when(pl.program_id(0) == 0)
    def _():
        outs[-1][...] = jnp.zeros_like(outs[-1])

    outs[-1][0:1, :] += jnp.sum(grad * hat, axis=0, keepdims=True)


def norm_back(order, which, own, sent, values, extra, gains, low):
    rows, width = own.shape
    spec = lines_spec(width)
    outs = [(spec, shaped((rows, width), F32))]
    outs += [(spec, shaped((rows, width), BF))] * low
    outs.append((pl.BlockSpec((8, width), lambda j, s: (0, 0)), shaped((8, width), F32)))
    return order.call(
        functools.partial(norm_back_kernel, which),
        (rows // LINES,),
        [spec, spec, spec, spec, held((2, width))],
        outs,
        (own, sent, values, extra, gains),
        work=8,
        name="norm_back",
    )


def sum_kernel(place_ref, *refs):
    refs[-1][...] = sum(r[...].astype(F32) for r in refs[:-1])


def sum_rows(order, *arrays):
    rows, width = arrays[0].shape
    spec = lines_spec(width)
    out = (spec, shaped((rows, width), F32))
    return order.call(sum_kernel, (rows // LINES,), [spec] * len(arrays), [out], arrays, work=4, name="sum_rows")[0]


def add_kernel(place_ref, *refs):
    at = 0
    for i in range(len(refs) // 2):
        a, b = refs[2 * i], refs[2 * i + 1]
        refs[-1][:, at : at + a.shape[1]] = (a[...].astype(F32) + b[...].astype(F32)).astype(BF)
        at += a.shape[1]


def add_pairs(order, pairs, skip=0, after=()):
    rows = pairs[0][1].shape[0]
    lines = min(LINES, rows)
    flat = [part for pair in pairs for part in pair]
    width = sum(a.shape[1] for a, _ in pairs)
    spec = lambda width, skip: pl.BlockSpec((lines, width), lambda j, s: (j + skip, 0))
    return order.call(
        add_kernel,
        (rows // lines,),
        [spec(a.shape[1], skip * (i == 0)) for pair in pairs for i, a in enumerate(pair)],
        [(spec(width, 0), shaped((rows, width), BF))],
        flat,
        after=after,
        work=5,
        name="add_pairs",
    )[0]


def take_kernel(place_ref, from_ref, out_ref):
    out_ref[...] = from_ref[...]


def take_rows(order, array):
    rows, width = array.shape
    block = pl.BlockSpec((rows // 2, width), lambda j, s: (0, 0))
    return order.call(
        take_kernel, (1,), [block], [(block, shaped((rows // 2, width), array.dtype))], [array], work=2, name="take_rows"
    )[0]


def adam_qkv_kernel(rate, place_ref, *refs):
    query, keyval, sums, query_out, keyval_out = refs[0:3], refs[3:6], refs[6], refs[7:10], refs[10:13]
    width = query[0].shape[1]
    new = adam_step(*[r[...] for r in query], sums[:, :width].astype(F32), rate, WEIGHT_DECAY)
    for out, value in zip(query_out, new, strict=True):
        out[...] = value
    for i in range(2):
        grad = sums[:, width + i * HD : width + (i + 1) * HD].astype(F32)
        new = adam_step(*[r[:, i, :] for r in keyval], grad, rate, WEIGHT_DECAY)
        for out, value in zip(keyval_out, new, strict=True):
            out[:, i, :] = value


def adam_qkv(order, query, keyval, sums, heads, rate):
    shard, wide = query[0].shape
    queries = pl.BlockSpec((shard, wide // heads), lambda j, s: (0, j))
    pair = pl.BlockSpec((shard, 2, HD), lambda j, s: (0, 0, j))
    return order.call(
        functools.partial(adam_qkv_kernel, rate),
        (heads,),
        [queries] * 3 + [pair] * 3 + [pl.BlockSpec((shard, wide // heads + 2 * HD), lambda j, s: (0, j))],
        [(queries, shaped(query[0].shape, F32))] * 3 + [(pair, shaped(keyval[0].shape, F32))] * 3,
        (*query, *keyval, sums),
        work=5,
        name="adam_qkv",
    )


def adam_out_kernel(rate, place_ref, *refs):
    new = adam_step(*[r[...] for r in refs[0:3]], refs[3][...].astype(F32).T, rate, WEIGHT_DECAY)
    for out, value in zip(refs[4:7], new, strict=True):
        out[...] = value


def adam_out(order, weights, sums, rate):
    tall, shard = weights[0].shape
    block = pl.BlockSpec((256, shard), lambda j, s: (j, 0))
    return order.call(
        functools.partial(adam_out_kernel, rate),
        (tall // 256,),
        [block] * 3 + [pl.BlockSpec((shard, 256), lambda j, s: (0, j))],
        [(block, shaped(weights[0].shape, F32))] * 3,
        (*weights, sums),
        work=3,
        name="adam_out",
    )


def adam_kernel(rates, place_ref, *refs):
    pair, down, all_sums, (pair_out, down_out), grad_ref = refs[0:3], refs[3:6], refs[6:-7], (refs[-7:-4], refs[-4:-1]), refs[-1]
    at = pl.program_id(0) // (pl.num_programs(0) // len(all_sums))
    sums = all_sums[0][...]
    for i in range(1, len(all_sums)):
        sums = jnp.where(at == i, all_sums[i][...], sums)
    sums = sums.astype(F32)
    down_grads = []
    for tile in range(2):
        first = tile * WIDE
        for piece in range(TILE // HD):
            for i in range(2):
                cols = slice(first + i * TILE + piece * HD, first + i * TILE + (piece + 1) * HD)
                grad_ref[:, tile * 4 + piece * 2 + i, :] = sums[:, cols]
        down_grads.append(sums[:, first + PAIR : first + WIDE].T)
    new = adam_step(*[r[...] for r in pair], grad_ref[...], rates[0], WEIGHT_DECAY)
    for out, value in zip(pair_out, new, strict=True):
        out[...] = value
    new = adam_step(*[r[...] for r in down], jnp.concatenate(down_grads, axis=0), rates[1], WEIGHT_DECAY)
    for out, value in zip(down_out, new, strict=True):
        out[...] = value


def adam_mlp(order, pair, down, sums, rates):
    shard, _, units = pair[0].shape
    rows = units // HD * 2
    seen = [v.reshape(shard, 2, units // HD, HD).transpose(0, 2, 1, 3).reshape(shard, rows, HD) for v in pair]
    wide = pl.BlockSpec((shard, 8, HD), lambda j, s: (0, j, 0))
    tall = pl.BlockSpec((2 * TILE, shard), lambda j, s: (j, 0))
    steps = units // TILE // len(sums) // 2
    part = lambda i: pl.BlockSpec((shard, 2 * WIDE), lambda j, s: (0, jnp.clip(j - i * steps, 0, steps - 1)))
    new = order.call(
        functools.partial(adam_kernel, rates),
        (units // TILE // 2,),
        [wide] * 3 + [tall] * 3 + [part(i) for i in range(len(sums))],
        [(wide, shaped(seen[0].shape, F32))] * 3 + [(tall, shaped(down[0].shape, F32))] * 3,
        (*seen, *down, *sums),
        scratch=[pltpu.VMEM((shard, 8, HD), F32)],
        work=20,
        name="adam_mlp",
    )
    back = lambda v: v.reshape(shard, units // HD, 2, HD).transpose(0, 2, 1, 3).reshape(shard, 2, units)
    return [*[back(v) for v in new[:3]], *new[3:]]


def rms_parts(values):
    return lax.rsqrt(jnp.mean(values * values, axis=-1, keepdims=True) + EPS_NORM)


def rope_tables(row_count):
    places = jnp.arange(row_count).astype(F32)
    inverse_freq = ROPE_BASE ** (-(jnp.arange(HD // 2).astype(F32) * 2.0) / HD)
    angles = places[:, None] * inverse_freq[None, :]
    sine = jnp.sin(angles)
    cosine = jnp.cos(angles)
    return jnp.concatenate([cosine, cosine], axis=1), jnp.concatenate([-sine, sine], axis=1)


def adam_step(weight, mean_old, square, gradient, step_rate, decay_rate):
    new_mean = BETA_ONE * mean_old + (1.0 - BETA_ONE) * gradient
    new_square = BETA_TWO * square + (1.0 - BETA_TWO) * gradient * gradient
    fix_one = 1.0 - BETA_ONE**STEP
    fix_two = 1.0 - BETA_TWO**STEP
    update = new_mean / fix_one / (jnp.sqrt(new_square / fix_two) + ADAM_EPS)
    return (weight - step_rate * (update + decay_rate * weight), new_mean, new_square)


class Summer:
    def __init__(self, axes, order, side):
        self.axes, self.order, self.side = axes, order, side
        self.lines = len(axes) == 3

    def other_core(self, piece):
        return lax.ppermute(piece, self.axes[2], [(0, 1), (1, 0)]) if self.lines else None

    def columns(self, own, other, in_order, after=()):
        if not self.lines:
            if not in_order:
                return jnp.concatenate([own, other], axis=0)
            first = self.side == 0
            return jnp.concatenate([jnp.where(first, own, other), jnp.where(first, other, own)], axis=0)
        keep, send = turn_columns(self.order, own, other, SIDE if in_order else None, self.axes, after)
        return keep, self.other_core(send)

    def whole(self, items):
        parts = []
        for left, (right, _), width, first, steps in items:
            right = right[:, first * width : (first + steps) * width]
            parts.append(mm(left, right, TN).astype(BF).reshape(left.shape[1], -1, width))
        return jnp.concatenate(parts, axis=2).reshape(parts[0].shape[0], -1)

    def grad(self, items, after=()):
        if not self.lines:
            return (self.whole(items),)
        near, keep = weight_grad(self.order, items, after=after)
        return keep, lax.ppermute(near, self.axes[1], [(0, 1), (1, 0)])

    def grad_by_line(self, items, after=()):
        if not self.lines:
            return self.finish((self.whole(items),))
        (whole,) = weight_grad(self.order, items, True, after)
        return lax.psum_scatter(whole, self.axes[0], scatter_dimension=0, tiled=True)

    def trade_by_line(self, summed):
        if not self.lines:
            return None
        return lax.ppermute(take_rows(self.order, summed), self.axes[1], [(0, 1), (1, 0)])

    def finish_by_line(self, summed, got):
        return add_pairs(self.order, [(summed, got)], 1) if self.lines else summed

    def finish(self, *grads, after=()):
        if not self.lines:
            return lax.psum_scatter(jnp.concatenate([g for g, in grads], axis=1), self.axes, scatter_dimension=0, tiled=True)
        line = add_pairs(self.order, grads, after=after)
        return lax.psum_scatter(line, self.axes[0], scatter_dimension=0, tiled=True)

    def everywhere(self, values):
        if not self.lines:
            return lax.psum(values, (*self.axes, "tensor"))
        pair = [(0, 1), (1, 0)]
        steps = [(self.axes[2], pair), (self.axes[1], pair)]
        steps += [(self.axes[0], [(0, 1), (1, 0), (2, 3), (3, 2)]), (self.axes[0], [(0, 2), (2, 0), (1, 3), (3, 1)])]
        for axis, pairs in (*steps, ("tensor", pair)):
            values = values + lax.ppermute(values, axis, pairs)
        return values


def on_device(
    axes,
    tokens,
    cotangent,
    lengths,
    w_query,
    query_mean,
    query_square,
    w_keyval,
    keyval_mean,
    keyval_square,
    w_out,
    out_mean,
    out_square,
    w_gateup,
    gateup_mean,
    gateup_square,
    w_down,
    down_mean,
    down_square,
    norm_gains,
    norm_mean,
    norm_square,
    head_gains,
    head_mean,
    head_square,
):
    side = lax.axis_index("tensor")
    tok_rows = tokens.shape[0]
    cap = 2 * tok_rows
    length = lengths[0]
    order = Order(side, length, lax.axis_index(axes[2]) if len(axes) == 3 else jnp.zeros_like(side))
    summer = Summer(axes, order, side)

    def swap(piece):
        return lax.ppermute(piece, "tensor", [(0, 1), (1, 0)])

    def there(*arrays):
        return [v for v in arrays if v is not None]

    def gather(shard):
        return lax.all_gather(shard, axes, axis=0, tiled=True)

    shard = w_query.shape[0]
    heads = w_keyval.shape[2] // HD
    group = w_query.shape[1] // HD // heads
    units = w_gateup.shape[2]
    tiles = units // TILE
    part = tiles // CHUNKS
    kv_low = w_keyval.astype(BF).reshape(shard, 2, heads, HD)
    qkv_shard = jnp.concatenate(
        [w_query.astype(BF).reshape(shard, heads, group * HD), kv_low[:, 0], kv_low[:, 1]], axis=2
    ).reshape(shard, heads * (group + 2) * HD)
    out_shard = w_out.astype(BF).T
    pair_low = w_gateup.astype(BF).reshape(shard, 2, tiles, TILE)
    down_low = w_down.astype(BF).T.reshape(shard, tiles, TILE)
    pair_low = jnp.stack([pair_low[:, 0], pair_low[:, 1]], axis=2).reshape(shard, CHUNKS, part * PAIR)
    down_low = down_low.reshape(shard, CHUNKS, part * TILE)
    mlp_shard = jnp.concatenate([pair_low, down_low], axis=2).reshape(shard, tiles * WIDE)

    stream = tokens.astype(F32)
    normed_own = (stream * rms_parts(stream) * norm_gains[0]).astype(BF)
    normed_other = swap(normed_own)
    qkv_cols, out_cols = qkv_shard.shape[1], out_shard.shape[1]
    early = gather(jnp.concatenate([qkv_shard, out_shard], axis=1))
    most = gather(mlp_shard[:, : (CHUNKS - 1) * part * WIDE])
    late = gather(mlp_shard[:, (CHUNKS - 1) * part * WIDE :])
    parts = [(most, part * p) for p in range(CHUNKS - 1)] + [(late, 0)]

    own_places = side * tok_rows + jnp.arange(tok_rows)
    live = (own_places < length)[:, None]
    back_own = jnp.where(live, cotangent, jnp.zeros_like(cotangent))
    back_other = swap(back_own)
    cosine, sine = rope_tables(cap)

    def there(*arrays):
        return [v for v in arrays if v is not None]

    normed_cols = summer.columns(normed_own, normed_other, True)

    qkv, attended = attend(order, normed_own, normed_other, early, cosine, sine, head_gains, heads, group)
    attended_core = summer.other_core(attended)
    out_pair = [(attended, 0, early, qkv_cols // BLOCK)]
    attended_sent = swap(contract(order, OTHER_SIDE, out_pair, BF))
    back_cols = summer.columns(back_own, back_other, False)
    attended_here = contract(order, SIDE, out_pair, F32, after=there(normed_cols[1], attended_core))
    middle, second_own = middle_rows(order, tokens, attended_here, attended_sent, norm_gains)

    second = (second_own, swap(second_own))
    back = (back_own, back_other)
    pair_blocks, down_blocks = part * PAIR // BLOCK, part * TILE // BLOCK
    part_blocks = pair_blocks + down_blocks

    def mlp(weights, count, after=(), through=()):
        grads, hidden, *handed = swiglu(order, second, back, weights, count, part, after, through)
        return ((grads, summer.other_core(grads)), (hidden, summer.other_core(hidden))), *handed

    def mlp_items(p):
        (grads, hidden), first = mlp_pieces[p // (CHUNKS - 1)], parts[p][1]
        return [(second_cols, grads, PAIR, first, part), (back_cols, hidden, TILE, first, part)]

    def second_pairs(p):
        (grads, _), weights, at = mlp_pieces[p // (CHUNKS - 1)], parts[p][0], parts[p][1] // part
        return [(grads[0], at * pair_blocks + b, weights, at * part_blocks + b) for b in range(pair_blocks)]

    def down_pairs(p):
        (_, hidden), weights, at = mlp_pieces[p // (CHUNKS - 1)], parts[p][0], parts[p][1] // part
        first = at * part_blocks + pair_blocks
        return [(hidden[0], at * down_blocks + b, weights, first + b) for b in range(down_blocks)]

    all_down = lambda: [pair for p in range(CHUNKS) for pair in down_pairs(p)]

    out_rows = early.shape[0] // 2
    core = order.scalars[CORE]
    out_half = lax.dynamic_slice(early, (core * out_rows, qkv_cols), (out_rows, out_cols))

    second_cols = summer.columns(*second, False)
    first_piece, out_half = mlp(most, CHUNKS - 1, there(back_cols[1]), [out_half])
    out_got = swap(out_half)
    mlp_pieces = [first_piece]
    d_second_part = contract(order, SECOND, second_pairs(0) + second_pairs(1), BF, after=there(second_cols[1]))
    line_sum = summer.grad_by_line(mlp_items(0))
    mlp_grads = [summer.grad(mlp_items(1))]
    last_piece, out_got = mlp(late, 1, through=[out_got])
    mlp_pieces.append(last_piece)
    d_second_sent = swap(contract(order, SECOND, second_pairs(2), BF, [d_second_part]))
    if summer.lines:
        out_other = [(out_got, 0, CORE), (summer.other_core(out_got), 0, OTHER_CORE)]
    else:
        out_other = [(swap(early[:, qkv_cols:]), 0, FIRST)]
    mlp_grads.append(summer.grad(mlp_items(2)))
    d_second = contract(order, FIRST, [pair for p in range(CHUNKS) for pair in second_pairs(p)], F32)
    d_middle, branch_own, branch_again, g_second_gain = norm_back(
        order, 1, d_second, d_second_sent, middle, back_own, norm_gains, 2
    )

    there_a, there_b = project(order, branch_own, out_other, out_cols)
    sent_a, sent_b = swap(there_a), swap(there_b)
    mlp_sums = [summer.finish(mlp_grads[0], after=[line_sum])]
    here_a, here_b, branch_again = project(
        order, branch_own, [(early, qkv_cols // out_cols, FIRST)], out_cols, [branch_again]
    )
    branch_other = swap(branch_again)

    def attention_back(half, here, sent, after=(), through=()):
        span = (half * heads // 2, heads // 2)
        d_part, g_part, *handed = attend_back(
            order, qkv, here, sent, cosine, sine, head_gains, span, group, after, through
        )
        return d_part, summer.other_core(d_part), g_part[:2], *handed

    d_qkv_a, core_a, g_head_a = attention_back(0, here_a, sent_a)
    d_qkv_b, core_b, g_head_b = attention_back(1, here_b, sent_b)
    qkv_grads = [
        summer.grad([(normed_cols, (d_qkv_a, core_a), 512, 0, d_qkv_a.shape[1] // 512)]),
        summer.grad([(normed_cols, (d_qkv_b, core_b), 512, 0, d_qkv_b.shape[1] // 512)]),
    ]
    mlp_sums.append(summer.finish(mlp_grads[1], after=mlp_sums[-1:]))
    line_got = summer.trade_by_line(line_sum)
    out_here, out_there = contract_both(order, FIRST, all_down())
    out_sent = swap(out_there)
    branch_cols = summer.columns(branch_again, branch_other, True)
    qkv_pairs = [(d_qkv_a, 0, early, 0), (d_qkv_b, 0, early, 1)]
    d_first, d_first_there = contract_both(order, SIDE, qkv_pairs)
    d_first_sent = swap(d_first_there)
    mlp_sums.insert(0, summer.finish_by_line(line_sum, line_got))
    qkv_sum = summer.finish(*qkv_grads, after=mlp_sums[-1:])
    out_grad = summer.grad([(branch_cols, (attended, attended_core), 512, 0, out_cols // 512)])
    wide_rate = RATE_SCALE * D ** (-0.5)
    mlp_new = adam_mlp(
        order,
        (w_gateup, gateup_mean, gateup_square),
        (w_down, down_mean, down_square),
        mlp_sums,
        (wide_rate, RATE_SCALE * FF ** (-0.5)),
    )
    out_sum = summer.finish(out_grad)
    order.rate = 0
    tokens_grad, g_first_gain = norm_back(order, 0, d_first, d_first_sent, tokens, d_middle, norm_gains, 0)
    qkv_new = adam_qkv(
        order, (w_query, query_mean, query_square), (w_keyval, keyval_mean, keyval_square), qkv_sum, heads, wide_rate
    )
    layer_out = sum_rows(order, middle, out_here, out_sent)
    out_new = adam_out(order, (w_out, out_mean, out_square), out_sum, RATE_SCALE * OUT_FAN ** (-0.5))
    g_head = g_head_a + g_head_b

    gains_here = jnp.concatenate([g_first_gain[0], g_second_gain[0], g_head.reshape(-1)]).reshape(-1, HD)
    gain_sums = summer.everywhere(gains_here).reshape(-1)
    norm_sum = gain_sums[: 2 * D].reshape(2, D)
    head_sum = gain_sums[2 * D :].reshape(2, HD)

    norm_new = adam_step(norm_gains, norm_mean, norm_square, norm_sum, GAIN_RATE, 0.0)
    head_new = adam_step(head_gains, head_mean, head_square, head_sum, GAIN_RATE, 0.0)
    return (layer_out, tokens_grad, *qkv_new, *out_new, *mlp_new, *norm_new, *head_new)


def solution(mesh):
    count, sides = mesh.shape["dp"], mesh.shape["tensor"]
    if count == 16:
        axes = ("z", "y", "core")
        grid = Mesh(mesh.devices.reshape(4, 2, 2, sides), (*axes, "tensor"))
    else:
        axes, grid = ("dp",), mesh
    rows = P((*axes, "tensor"), None)
    in_out = [P(axes, "tensor")] * 3 + [P(axes, None, "tensor")] * 3 + [P("tensor", axes)] * 3
    in_out += [P(axes, None, "tensor")] * 3 + [P("tensor", axes)] * 3 + [P()] * 6
    return jax.shard_map(
        functools.partial(on_device, axes),
        mesh=grid,
        in_specs=(rows, rows, P(axes), *in_out),
        out_specs=(rows, rows, *in_out),
        check_vma=False,
    )
```

```python
import functools

import jax
import jax.numpy as jnp
from jax import lax
from jax.experimental import pallas as pl
from jax.experimental.pallas import tpu as pltpu
from jax.sharding import Mesh
from jax.sharding import PartitionSpec as P

D = 2048
HD = 128
FF = 6144
STEP = 10
LEN_MIN = 640

EPS_NORM = 1e-06
ROPE_BASE = 1000000.0
BETA_ONE = 0.9
BETA_TWO = 0.95
ADAM_EPS = 1e-08
WEIGHT_DECAY = 0.1
RATE_SCALE = 2.0
GAIN_RATE = 0.6
OUT_FAN = 8.0
LOG2_E = 1.4426950408889634

BF = jnp.bfloat16
F32 = jnp.float32
ROWS = 256
TILE = 256
BLOCK = 1024
CHUNKS = 3
WORK = 10**10

NN = (((1,), (0,)), ((), ()))
NT = (((1,), (1,)), ((), ()))
TN = (((0,), (0,)), ((), ()))


def mm(a, b, dims=NN):
    return lax.dot_general(a, b, dims, preferred_element_type=F32)


class Order:
    def __init__(self, side, length, core):
        self.rate = WORK
        one = jnp.ones_like(side)
        self.scalars = jnp.stack([side, 1 - side, length, 0 * one, one, core, 1 - core]).astype(jnp.int32)

    def call(self, kernel, grid, ins, outs, operands, *, after=(), through=(), vmem=48, scratch=(), work, name):
        count, later, made = len(ins), len(after) + len(through), len(outs)
        anywhere = pl.BlockSpec(memory_space=pl.ANY)

        def run(scalars, *refs):
            first = count + later
            token = refs[first + made]
            for i in range(token.shape[0]):
                token[i] = scalars[i]
            kernel(scalars, *refs[:count], *refs[first : first + made], *refs[first + made + 1 + len(through) :])

        results = pl.pallas_call(
            run,
            grid_spec=pltpu.PrefetchScalarGridSpec(
                num_scalar_prefetch=1,
                grid=grid,
                in_specs=[*ins, *[anywhere] * later],
                out_specs=[spec for spec, _ in outs] + [pl.BlockSpec(memory_space=pltpu.SMEM)] + [anywhere] * len(through),
                scratch_shapes=scratch,
            ),
            out_shape=[shape for _, shape in outs]
            + [shaped(self.scalars.shape, jnp.int32)]
            + [shaped(v.shape, v.dtype) for v in through],
            input_output_aliases={1 + count + len(after) + i: made + 1 + i for i in range(len(through))},
            compiler_params=pltpu.CompilerParams(vmem_limit_bytes=vmem * 2**20),
            cost_estimate=pl.CostEstimate(flops=int(work * self.rate) + 1, bytes_accessed=1, transcendentals=0),
            name=name,
        )(self.scalars, *operands, *after, *through)
        self.scalars = results[made]
        return results[:made] + results[made + 1 :]


SIDE, OTHER_SIDE, LENGTH, FIRST, SECOND, CORE, OTHER_CORE = range(7)


def shaped(shape, dtype):
    return jax.ShapeDtypeStruct(shape, dtype)


def held(shape):
    return pl.BlockSpec(shape, lambda *_: (0,) * len(shape), pipeline_mode=pl.Buffered(1))


def turn(values, gain, cosine, sine):
    scale = lax.rsqrt(jnp.mean(values * values, axis=-1, keepdims=True) + EPS_NORM)
    normed = values * scale * gain
    return normed * cosine + pltpu.roll(normed, HD // 2, 1) * sine


def turn_back(grad, values, gain, cosine, sine):
    scale = lax.rsqrt(jnp.mean(values * values, axis=-1, keepdims=True) + EPS_NORM)
    d_normed = grad * cosine + pltpu.roll(grad * sine, HD // 2, 1)
    hat = values * scale
    d_gain = jnp.sum(d_normed * hat, axis=0, keepdims=True)
    d_hat = d_normed * gain
    inner = jnp.mean(d_hat * hat, axis=-1, keepdims=True)
    return scale * (d_hat - hat * inner), d_gain


def key_spans(block):
    start = block * ROWS
    free = min(start, LEN_MIN // ROWS * ROWS)
    spans = []
    if free:
        spans.append((0, free, False, False))
    if start > free:
        spans.append((free, start, False, True))
    spans.append((start, start + ROWS, True, start + ROWS > LEN_MIN))
    return spans


def raised_scores(query, keys, span, length):
    first, last, causal, ragged = span
    scores = mm(query, keys[first:last], NT) * (HD**-0.5 * LOG2_E)
    raised = jnp.exp2(scores)
    allowed = None
    shape = raised.shape
    if causal:
        place = lax.broadcasted_iota(jnp.int32, shape, 0) % ROWS
        allowed = lax.broadcasted_iota(jnp.int32, shape, 1) <= place
    if ragged:
        live = lax.broadcasted_iota(jnp.int32, shape, 1) + first < length
        allowed = live if allowed is None else allowed & live
    return raised if allowed is None else jnp.where(allowed, raised, 0.0)


def split_heads(qkv_ref, group):
    width = group * HD
    queries = [qkv_ref[:, h * HD : (h + 1) * HD] for h in range(group)]
    return queries, qkv_ref[:, width : width + HD], qkv_ref[:, width + HD : width + 2 * HD]


def attend_kernel(group, place_ref, own_ref, other_ref, weight_ref, cos_ref, sin_ref, gain_ref, qkv_ref, out_ref):
    side, length = place_ref[SIDE], place_ref[LENGTH]
    half = own_ref.shape[0]
    qkv_ref[pl.ds(pl.multiple_of(side * half, half), half), :] = mm(own_ref[...], weight_ref[...])
    qkv_ref[pl.ds(pl.multiple_of((1 - side) * half, half), half), :] = mm(other_ref[...], weight_ref[...])
    cosine, sine = cos_ref[...], sin_ref[...]
    queries, keys, values = split_heads(qkv_ref, group)
    turned = [turn(q, gain_ref[0:1], cosine, sine).astype(BF) for q in queries]
    keys = turn(keys, gain_ref[1:2], cosine, sine).astype(BF)
    values = values.astype(BF)
    for block in range(qkv_ref.shape[0] // ROWS):
        rows = slice(block * ROWS, (block + 1) * ROWS)
        query = jnp.concatenate([t[rows] for t in turned], axis=0)
        total, mixed = 0.0, 0.0
        for span in key_spans(block):
            raised = raised_scores(query, keys, span, length)
            total = total + jnp.sum(raised, axis=-1, keepdims=True)
            mixed = mixed + mm(raised.astype(BF), values[span[0] : span[1]])
        mixed = (mixed / total).astype(BF)
        for h in range(group):
            out_ref[rows, h * HD : (h + 1) * HD] = mixed[h * ROWS : (h + 1) * ROWS]


def attend_back_kernel(
    group,
    place_ref,
    qkv_ref,
    own_ref,
    other_ref,
    cos_ref,
    sin_ref,
    gain_ref,
    out_ref,
    gain_out,
    grad_ref,
    dk_ref,
    dv_ref,
):
    side, length = place_ref[SIDE], place_ref[LENGTH]
    half = own_ref.shape[0]
    grad_ref[pl.ds(pl.multiple_of(side * half, half), half), :] = own_ref[...]
    grad_ref[pl.ds(pl.multiple_of((1 - side) * half, half), half), :] = other_ref[...]
    cosine, sine = cos_ref[...], sin_ref[...]
    queries, raw_keys, values = split_heads(qkv_ref, group)
    turned = [turn(q, gain_ref[0:1], cosine, sine).astype(BF) for q in queries]
    keys = turn(raw_keys, gain_ref[1:2], cosine, sine).astype(BF)
    values = values.astype(BF)
    dk_ref[...] = jnp.zeros_like(dk_ref)
    dv_ref[...] = jnp.zeros_like(dv_ref)
    q_gain = jnp.zeros((1, HD), F32)
    for block in range(qkv_ref.shape[0] // ROWS):
        rows = slice(block * ROWS, (block + 1) * ROWS)
        query = jnp.concatenate([t[rows] for t in turned], axis=0)
        grad = jnp.concatenate([grad_ref[rows, h * HD : (h + 1) * HD] for h in range(group)], axis=0)
        spans = key_spans(block)
        raised = [raised_scores(query, keys, span, length) for span in spans]
        total = sum(jnp.sum(r, axis=-1, keepdims=True) for r in raised)
        fix = 1.0 / total
        chances = [r * fix for r in raised]
        d_chances = [mm(grad, values[s[0] : s[1]], NT) for s in spans]
        inner = sum(jnp.sum(c * d, axis=-1, keepdims=True) for c, d in zip(chances, d_chances, strict=True))
        d_query = 0.0
        for span, chance, d_chance in zip(spans, chances, d_chances, strict=True):
            d_score = (chance * (d_chance - inner) * (HD**-0.5)).astype(BF)
            part = slice(span[0], span[1])
            d_query = d_query + mm(d_score, keys[part])
            dk_ref[part, :] += mm(d_score, query, TN)
            dv_ref[part, :] += mm(chance.astype(BF), grad, TN)
        for h in range(group):
            cols = slice(h * HD, (h + 1) * HD)
            d_raw, d_gain = turn_back(
                d_query[h * ROWS : (h + 1) * ROWS], qkv_ref[rows, cols], gain_ref[0:1], cosine[rows], sine[rows]
            )
            out_ref[rows, cols] = d_raw.astype(BF)
            q_gain = q_gain + d_gain
    width = group * HD
    d_raw, k_gain = turn_back(dk_ref[...], raw_keys, gain_ref[1:2], cosine, sine)
    out_ref[:, width : width + HD] = d_raw.astype(BF)
    out_ref[:, width + HD : width + 2 * HD] = dv_ref[...].astype(BF)

    @pl.when(pl.program_id(0) == 0)
    def _():
        gain_out[...] = jnp.zeros_like(gain_out)

    gain_out[0:1, :] += q_gain
    gain_out[1:2, :] += k_gain


def attend(order, own, other, weights, cosine, sine, gains, heads, group):
    half, width = own.shape
    cap, cols = 2 * half, (group + 2) * HD
    return order.call(
        functools.partial(attend_kernel, group),
        (heads,),
        [
            held((half, width)),
            held((half, width)),
            pl.BlockSpec((width, cols), lambda n, s: (0, n)),
            held((cap, HD)),
            held((cap, HD)),
            held((2, HD)),
        ],
        [
            (pl.BlockSpec((cap, cols), lambda n, s: (0, n)), shaped((cap, heads * cols), F32)),
            (pl.BlockSpec((cap, group * HD), lambda n, s: (0, n)), shaped((cap, heads * group * HD), BF)),
        ],
        (own, other, weights, cosine, sine, gains),
        work=24,
        name="attend",
    )


def attend_back(order, qkv, own, other, cosine, sine, gains, span, group, after=(), through=()):
    half, cap, cols = own.shape[0], 2 * own.shape[0], (group + 2) * HD
    first, heads = span
    rows = pl.BlockSpec((half, group * HD), lambda n, s: (0, n))
    return order.call(
        functools.partial(attend_back_kernel, group),
        (heads,),
        [
            pl.BlockSpec((cap, cols), lambda n, s: (0, first + n)),
            rows,
            rows,
            held((cap, HD)),
            held((cap, HD)),
            held((2, HD)),
        ],
        [
            (pl.BlockSpec((cap, cols), lambda n, s: (0, n)), shaped((cap, heads * cols), BF)),
            (pl.BlockSpec((8, HD), lambda n, s: (0, 0)), shaped((8, HD), F32)),
        ],
        (qkv, own, other, cosine, sine, gains),
        after=after,
        through=through,
        scratch=[pltpu.VMEM((cap, group * HD), BF), pltpu.VMEM((cap, HD), F32), pltpu.VMEM((cap, HD), F32)],
        work=17,
        name="attend_back",
    )


def project_kernel(count, place_ref, *refs):
    for out_ref, at in ((refs[-2], 0), (refs[-1], refs[-2].shape[1])):
        cols = slice(at, at + out_ref.shape[1])
        out_ref[...] = sum(mm(refs[i][...], refs[count + i][:, cols]) for i in range(count)).astype(BF)


def project(order, rows, weights, cols, through=()):
    half, depth = rows.shape[0], weights[0][0].shape[0]
    left = [pl.BlockSpec((half, depth), functools.partial(lambda at, j, s: (0, s[at]), at)) for _, _, at in weights]
    right = [pl.BlockSpec((depth, cols), functools.partial(lambda at, j, s: (0, at), at)) for _, at, _ in weights]
    out = pl.BlockSpec((half, cols // 2), lambda j, s: (0, 0))
    return order.call(
        functools.partial(project_kernel, len(weights)),
        (1,),
        left + right,
        [(out, shaped((half, cols // 2), BF))] * 2,
        (*[rows] * len(weights), *[w for w, _, _ in weights]),
        through=through,
        work=5,
        name="project",
    )


WIDE = 3 * TILE
PAIR = 2 * TILE


def swiglu_kernel(place_ref, second_own, second_other, back_own, back_other, pair_ref, down_ref, grad_ref, hidden_ref):
    half = second_own.shape[0]
    for at, second_ref, back_ref in ((0, second_own, back_own), (half, second_other, back_other)):
        rows = slice(at, at + half)
        pair = mm(second_ref[...], pair_ref[...])
        d_hidden = mm(back_ref[...], down_ref[...])
        gate, up = pair[:, :TILE], pair[:, TILE:]
        sigmoid = 1.0 / (1.0 + jnp.exp(-gate))
        silu = gate * sigmoid
        d_gate = d_hidden * up * (sigmoid * (1.0 + gate * (1.0 - sigmoid)))
        grad_ref[rows, :TILE] = d_gate.astype(BF)
        grad_ref[rows, TILE:] = (d_hidden * silu).astype(BF)
        hidden_ref[rows, :] = (silu * up).astype(BF)


def swiglu(order, second, back, weights, count, tiles, after=(), through=()):
    half, width = second[0].shape
    rows = held((half, width))
    pair_at = lambda j: j // tiles * (3 * tiles // 2) + j % tiles
    down_at = lambda j: j // tiles * (3 * tiles) + 2 * tiles + j % tiles
    return order.call(
        swiglu_kernel,
        (count * tiles,),
        [
            rows,
            rows,
            rows,
            rows,
            pl.BlockSpec((width, PAIR), lambda j, s: (0, pair_at(j))),
            pl.BlockSpec((width, TILE), lambda j, s: (0, down_at(j))),
        ],
        [
            (pl.BlockSpec((2 * half, PAIR), lambda j, s: (0, j)), shaped((2 * half, count * tiles * PAIR), BF)),
            (pl.BlockSpec((2 * half, TILE), lambda j, s: (0, j)), shaped((2 * half, count * tiles * TILE), BF)),
        ],
        (*second, *back, weights, weights),
        after=after,
        through=through,
        work=5 * count * tiles,
        name="swiglu",
    )


def turn_columns_kernel(which, place_ref, own_keep, other_keep, own_send, other_send, keep_ref, send_ref):
    half = own_keep.shape[0]
    if which is None:
        own_at, other_at = slice(0, half), slice(half, 2 * half)
    else:
        own_at = pl.ds(pl.multiple_of(place_ref[which] * half, half), half)
        other_at = pl.ds(pl.multiple_of((1 - place_ref[which]) * half, half), half)
    keep_ref[:, own_at] = own_keep[...].T
    keep_ref[:, other_at] = other_keep[...].T
    send_ref[:, own_at] = own_send[...].T
    send_ref[:, other_at] = other_send[...].T


def turn_columns(order, own, other, which, axes, after=()):
    half = own.shape[0]
    owned = own.shape[1] // 16
    y, c = lax.axis_index(axes[1]), lax.axis_index(axes[2])
    at = lambda j, mine: (j % 4) * 4 + jnp.where(j < 4, 1 - y, y) * 2 + jnp.where(mine, c, 1 - c)
    lines = jnp.arange(8, dtype=jnp.int32)
    table = jnp.concatenate([at(lines, True), at(lines, False)]).astype(jnp.int32)
    scalars = jnp.concatenate([order.scalars, table])
    base = order.scalars.shape[0]
    keep = pl.BlockSpec((half, owned), lambda j, s: (0, s[base + j]))
    send = pl.BlockSpec((half, owned), lambda j, s: (0, s[base + 8 + j]))
    out = pl.BlockSpec((owned, 2 * half), lambda j, s: (j, 0))
    held_back, order.scalars = order.scalars, scalars
    keep_cols, send_cols = order.call(
        functools.partial(turn_columns_kernel, which),
        (8,),
        [keep, keep, send, send],
        [(out, shaped((8 * owned, 2 * half), BF))] * 2,
        (own, other, own, other),
        after=after,
        work=7,
        name="turn_columns",
    )
    order.scalars = order.scalars[:base]
    return keep_cols, send_cols


def weight_grad_kernel(widths, place_ref, *refs):
    outs = refs[4 * len(widths) :]
    half = refs[0].shape[0] // 2
    first = 0
    for i, width in enumerate(widths):
        left, far_left, right, far_right = refs[4 * i : 4 * i + 4]
        cols = slice(first, first + width)
        first += width
        product = mm(left[...], right[...]) + mm(far_left[...], far_right[...])
        if len(outs) == 2:
            outs[0][:, cols] = product[:half].astype(BF)
            outs[1][:, cols] = product[half:].astype(BF)
            continue
        for line in range(4):
            at, owned = line * half // 2, half // 4
            outs[0][at : at + owned, cols] = product[line * owned : (line + 1) * owned].astype(BF)
            outs[0][at + owned : at + 2 * owned, cols] = product[half + line * owned : half + (line + 1) * owned].astype(BF)


def weight_grad(order, items, by_line=False, after=()):
    rows, cap = items[0][0][0].shape
    widths = [width for _, _, width, _, _ in items]
    steps, step = items[0][4], sum(widths)
    out_rows = rows if by_line else rows // 2
    out = (pl.BlockSpec((out_rows, step), lambda j, s: (0, j)), shaped((out_rows, steps * step), BF))
    ins = []
    for _, _, width, first, _ in items:
        ins += [held((rows, cap))] * 2
        ins += [pl.BlockSpec((cap, width), functools.partial(lambda first, j, s: (0, first + j), first))] * 2
    return order.call(
        functools.partial(weight_grad_kernel, widths),
        (steps,),
        ins,
        [out] if by_line else [out, out],
        [part for left, right, *_ in items for part in (*left, *right)],
        after=after,
        work=steps * step // 160,
        name="weight_grad",
    )


def contract_kernel(count, adds, place_ref, *refs):
    total = 0.0
    for i in range(count):
        total = total + mm(refs[i][...], refs[count + i][...], NT)
    for i in range(adds):
        total = total + refs[2 * count + i][...].astype(F32)
    refs[-1][...] = total.astype(refs[-1].dtype)


def contract(order, which, pairs, dtype, adds=(), after=()):
    half, width = pairs[0][0].shape[0] // 2, pairs[0][2].shape[0]
    step = 512
    ins = [
        pl.BlockSpec((half, BLOCK), functools.partial(lambda at, j, s: (s[which], at), at), pipeline_mode=pl.Buffered(1))
        for _, at, _, _ in pairs
    ]
    ins += [pl.BlockSpec((step, BLOCK), functools.partial(lambda at, j, s: (j, at), at)) for _, _, _, at in pairs]
    across = pl.BlockSpec((half, step), lambda j, s: (0, j))
    return order.call(
        functools.partial(contract_kernel, len(pairs), len(adds)),
        (width // step,),
        ins + [across] * len(adds),
        [(across, shaped((half, width), dtype))],
        (*[left for left, _, _, _ in pairs], *[weights for _, _, weights, _ in pairs], *adds),
        after=after,
        work=8 * len(pairs),
        name="contract",
    )[0]


def contract_both_kernel(which, count, place_ref, *refs):
    total = 0.0
    for i in range(count):
        total = total + mm(refs[i][...], refs[count + i][...], NT)
    half = total.shape[0] // 2
    first, second = total[:half], total[half:]
    here_ref, there_ref = refs[-2:]
    if which == FIRST:
        here_ref[...], there_ref[...] = first, second.astype(BF)
        return
    here = place_ref[which] == 0
    here_ref[...] = jnp.where(here, first, second)
    there_ref[...] = jnp.where(here, second, first).astype(BF)


def contract_both(order, which, pairs):
    rows, width = pairs[0][0].shape[0], pairs[0][2].shape[0]
    step = 512
    ins = [
        pl.BlockSpec((rows, BLOCK), functools.partial(lambda at, j, s: (0, at), at), pipeline_mode=pl.Buffered(1))
        for _, at, _, _ in pairs
    ]
    ins += [pl.BlockSpec((step, BLOCK), functools.partial(lambda at, j, s: (j, at), at)) for _, _, _, at in pairs]
    across = pl.BlockSpec((rows // 2, step), lambda j, s: (0, j))
    return order.call(
        functools.partial(contract_both_kernel, which, len(pairs)),
        (width // step,),
        ins,
        [(across, shaped((rows // 2, width), F32)), (across, shaped((rows // 2, width), BF))],
        (*[left for left, _, _, _ in pairs], *[weights for _, _, weights, _ in pairs]),
        work=5 * len(pairs),
        name="contract_both",
    )


LINES = 128


def lines_spec(width):
    return pl.BlockSpec((LINES, width), lambda j, s: (j, 0))


def middle_kernel(place_ref, tokens_ref, own_ref, sent_ref, gain_ref, middle_ref, second_ref):
    middle = tokens_ref[...].astype(F32) + own_ref[...] + sent_ref[...].astype(F32)
    middle_ref[...] = middle
    second_ref[...] = (middle * rms_parts(middle) * gain_ref[1:2, :]).astype(BF)


def middle_rows(order, tokens, own, sent, gains, after=()):
    rows, width = tokens.shape
    spec = lines_spec(width)
    return order.call(
        middle_kernel,
        (rows // LINES,),
        [spec, spec, spec, held((2, width))],
        [(spec, shaped((rows, width), F32)), (spec, shaped((rows, width), BF))],
        (tokens, own, sent, gains),
        after=after,
        work=6,
        name="middle_rows",
    )


def norm_back_kernel(which, place_ref, own_ref, sent_ref, value_ref, extra_ref, gain_ref, *outs):
    grad = own_ref[...] + sent_ref[...].astype(F32)
    values = value_ref[...].astype(F32)
    scale = rms_parts(values)
    hat = values * scale
    d_hat = grad * gain_ref[which : which + 1, :]
    inner = jnp.mean(d_hat * hat, axis=-1, keepdims=True)
    total = extra_ref[...].astype(F32) + scale * (d_hat - hat * inner)
    outs[0][...] = total
    for out in outs[1:-1]:
        out[...] = total.astype(BF)

    @pl.when(pl.program_id(0) == 0)
    def _():
        outs[-1][...] = jnp.zeros_like(outs[-1])

    outs[-1][0:1, :] += jnp.sum(grad * hat, axis=0, keepdims=True)


def norm_back(order, which, own, sent, values, extra, gains, low):
    rows, width = own.shape
    spec = lines_spec(width)
    outs = [(spec, shaped((rows, width), F32))]
    outs += [(spec, shaped((rows, width), BF))] * low
    outs.append((pl.BlockSpec((8, width), lambda j, s: (0, 0)), shaped((8, width), F32)))
    return order.call(
        functools.partial(norm_back_kernel, which),
        (rows // LINES,),
        [spec, spec, spec, spec, held((2, width))],
        outs,
        (own, sent, values, extra, gains),
        work=8,
        name="norm_back",
    )


def sum_kernel(place_ref, *refs):
    refs[-1][...] = sum(r[...].astype(F32) for r in refs[:-1])


def sum_rows(order, *arrays):
    rows, width = arrays[0].shape
    spec = lines_spec(width)
    out = (spec, shaped((rows, width), F32))
    return order.call(sum_kernel, (rows // LINES,), [spec] * len(arrays), [out], arrays, work=4, name="sum_rows")[0]


def add_kernel(place_ref, *refs):
    at = 0
    for i in range(len(refs) // 2):
        a, b = refs[2 * i], refs[2 * i + 1]
        refs[-1][:, at : at + a.shape[1]] = (a[...].astype(F32) + b[...].astype(F32)).astype(BF)
        at += a.shape[1]


def add_pairs(order, pairs, skip=0, after=()):
    rows = pairs[0][1].shape[0]
    lines = min(LINES, rows)
    flat = [part for pair in pairs for part in pair]
    width = sum(a.shape[1] for a, _ in pairs)
    spec = lambda width, skip: pl.BlockSpec((lines, width), lambda j, s: (j + skip, 0))
    return order.call(
        add_kernel,
        (rows // lines,),
        [spec(a.shape[1], skip * (i == 0)) for pair in pairs for i, a in enumerate(pair)],
        [(spec(width, 0), shaped((rows, width), BF))],
        flat,
        after=after,
        work=5,
        vmem=62, name="add_pairs",
    )[0]


def take_kernel(place_ref, from_ref, out_ref):
    out_ref[...] = from_ref[...]


def take_rows(order, array):
    rows, width = array.shape
    block = pl.BlockSpec((rows // 2, width), lambda j, s: (0, 0))
    return order.call(
        take_kernel, (1,), [block], [(block, shaped((rows // 2, width), array.dtype))], [array], work=2, vmem=62, name="take_rows"
    )[0]


def adam_qkv_kernel(rate, place_ref, *refs):
    query, keyval, sums, query_out, keyval_out = refs[0:3], refs[3:6], refs[6], refs[7:10], refs[10:13]
    width = query[0].shape[1]
    new = adam_step(*[r[...] for r in query], sums[:, :width].astype(F32), rate, WEIGHT_DECAY)
    for out, value in zip(query_out, new, strict=True):
        out[...] = value
    for i in range(2):
        grad = sums[:, width + i * HD : width + (i + 1) * HD].astype(F32)
        new = adam_step(*[r[:, i, :] for r in keyval], grad, rate, WEIGHT_DECAY)
        for out, value in zip(keyval_out, new, strict=True):
            out[:, i, :] = value


def adam_qkv(order, query, keyval, sums, heads, rate):
    shard, wide = query[0].shape
    queries = pl.BlockSpec((shard, wide // heads), lambda j, s: (0, j))
    pair = pl.BlockSpec((shard, 2, HD), lambda j, s: (0, 0, j))
    return order.call(
        functools.partial(adam_qkv_kernel, rate),
        (heads,),
        [queries] * 3 + [pair] * 3 + [pl.BlockSpec((shard, wide // heads + 2 * HD), lambda j, s: (0, j))],
        [(queries, shaped(query[0].shape, F32))] * 3 + [(pair, shaped(keyval[0].shape, F32))] * 3,
        (*query, *keyval, sums),
        work=5,
        vmem=62, name="adam_qkv",
    )


def adam_out_kernel(rate, place_ref, *refs):
    new = adam_step(*[r[...] for r in refs[0:3]], refs[3][...].astype(F32).T, rate, WEIGHT_DECAY)
    for out, value in zip(refs[4:7], new, strict=True):
        out[...] = value


def adam_out(order, weights, sums, rate):
    tall, shard = weights[0].shape
    block = pl.BlockSpec((256, shard), lambda j, s: (j, 0))
    return order.call(
        functools.partial(adam_out_kernel, rate),
        (tall // 256,),
        [block] * 3 + [pl.BlockSpec((shard, 256), lambda j, s: (0, j))],
        [(block, shaped(weights[0].shape, F32))] * 3,
        (*weights, sums),
        work=3,
        vmem=62, name="adam_out",
    )


def adam_kernel(rates, place_ref, *refs):
    pair, down, all_sums, (pair_out, down_out), grad_ref = refs[0:3], refs[3:6], refs[6:-7], (refs[-7:-4], refs[-4:-1]), refs[-1]
    at = pl.program_id(0) // (pl.num_programs(0) // len(all_sums))
    sums = all_sums[0][...]
    for i in range(1, len(all_sums)):
        sums = jnp.where(at == i, all_sums[i][...], sums)
    sums = sums.astype(F32)
    down_grads = []
    for tile in range(2):
        first = tile * WIDE
        for piece in range(TILE // HD):
            for i in range(2):
                cols = slice(first + i * TILE + piece * HD, first + i * TILE + (piece + 1) * HD)
                grad_ref[:, tile * 4 + piece * 2 + i, :] = sums[:, cols]
        down_grads.append(sums[:, first + PAIR : first + WIDE].T)
    new = adam_step(*[r[...] for r in pair], grad_ref[...], rates[0], WEIGHT_DECAY)
    for out, value in zip(pair_out, new, strict=True):
        out[...] = value
    new = adam_step(*[r[...] for r in down], jnp.concatenate(down_grads, axis=0), rates[1], WEIGHT_DECAY)
    for out, value in zip(down_out, new, strict=True):
        out[...] = value


def adam_mlp(order, pair, down, sums, rates):
    shard, _, units = pair[0].shape
    rows = units // HD * 2
    seen = [v.reshape(shard, 2, units // HD, HD).transpose(0, 2, 1, 3).reshape(shard, rows, HD) for v in pair]
    wide = pl.BlockSpec((shard, 8, HD), lambda j, s: (0, j, 0))
    tall = pl.BlockSpec((2 * TILE, shard), lambda j, s: (j, 0))
    steps = units // TILE // len(sums) // 2
    part = lambda i: pl.BlockSpec((shard, 2 * WIDE), lambda j, s: (0, jnp.clip(j - i * steps, 0, steps - 1)))
    new = order.call(
        functools.partial(adam_kernel, rates),
        (units // TILE // 2,),
        [wide] * 3 + [tall] * 3 + [part(i) for i in range(len(sums))],
        [(wide, shaped(seen[0].shape, F32))] * 3 + [(tall, shaped(down[0].shape, F32))] * 3,
        (*seen, *down, *sums),
        scratch=[pltpu.VMEM((shard, 8, HD), F32)],
        work=20,
        name="adam_mlp",
    )
    back = lambda v: v.reshape(shard, units // HD, 2, HD).transpose(0, 2, 1, 3).reshape(shard, 2, units)
    return [*[back(v) for v in new[:3]], *new[3:]]


def rms_parts(values):
    return lax.rsqrt(jnp.mean(values * values, axis=-1, keepdims=True) + EPS_NORM)


def rope_tables(row_count):
    places = jnp.arange(row_count).astype(F32)
    inverse_freq = ROPE_BASE ** (-(jnp.arange(HD // 2).astype(F32) * 2.0) / HD)
    angles = places[:, None] * inverse_freq[None, :]
    sine = jnp.sin(angles)
    cosine = jnp.cos(angles)
    return jnp.concatenate([cosine, cosine], axis=1), jnp.concatenate([-sine, sine], axis=1)


def adam_step(weight, mean_old, square, gradient, step_rate, decay_rate):
    new_mean = BETA_ONE * mean_old + (1.0 - BETA_ONE) * gradient
    new_square = BETA_TWO * square + (1.0 - BETA_TWO) * gradient * gradient
    fix_one = 1.0 - BETA_ONE**STEP
    fix_two = 1.0 - BETA_TWO**STEP
    update = new_mean / fix_one / (jnp.sqrt(new_square / fix_two) + ADAM_EPS)
    return (weight - step_rate * (update + decay_rate * weight), new_mean, new_square)


class Summer:
    def __init__(self, axes, order, side):
        self.axes, self.order, self.side = axes, order, side
        self.lines = len(axes) == 3

    def other_core(self, piece):
        return lax.ppermute(piece, self.axes[2], [(0, 1), (1, 0)]) if self.lines else None

    def columns(self, own, other, in_order, after=()):
        if not self.lines:
            if not in_order:
                return jnp.concatenate([own, other], axis=0)
            first = self.side == 0
            return jnp.concatenate([jnp.where(first, own, other), jnp.where(first, other, own)], axis=0)
        keep, send = turn_columns(self.order, own, other, SIDE if in_order else None, self.axes, after)
        return keep, self.other_core(send)

    def whole(self, items):
        parts = []
        for left, (right, _), width, first, steps in items:
            right = right[:, first * width : (first + steps) * width]
            parts.append(mm(left, right, TN).astype(BF).reshape(left.shape[1], -1, width))
        return jnp.concatenate(parts, axis=2).reshape(parts[0].shape[0], -1)

    def grad(self, items, after=()):
        if not self.lines:
            return (self.whole(items),)
        near, keep = weight_grad(self.order, items, after=after)
        return keep, lax.ppermute(near, self.axes[1], [(0, 1), (1, 0)])

    def grad_by_line(self, items, after=()):
        if not self.lines:
            return self.finish((self.whole(items),))
        (whole,) = weight_grad(self.order, items, True, after)
        return lax.psum_scatter(whole, self.axes[0], scatter_dimension=0, tiled=True)

    def trade_by_line(self, summed):
        if not self.lines:
            return None
        return lax.ppermute(take_rows(self.order, summed), self.axes[1], [(0, 1), (1, 0)])

    def finish_by_line(self, summed, got):
        return add_pairs(self.order, [(summed, got)], 1) if self.lines else summed

    def finish(self, *grads, after=()):
        if not self.lines:
            return lax.psum_scatter(jnp.concatenate([g for g, in grads], axis=1), self.axes, scatter_dimension=0, tiled=True)
        line = add_pairs(self.order, grads, after=after)
        return lax.psum_scatter(line, self.axes[0], scatter_dimension=0, tiled=True)

    def everywhere(self, values):
        if not self.lines:
            return lax.psum(values, (*self.axes, "tensor"))
        pair = [(0, 1), (1, 0)]
        steps = [(self.axes[2], pair), (self.axes[1], pair)]
        steps += [(self.axes[0], [(0, 1), (1, 0), (2, 3), (3, 2)]), (self.axes[0], [(0, 2), (2, 0), (1, 3), (3, 1)])]
        for axis, pairs in (*steps, ("tensor", pair)):
            values = values + lax.ppermute(values, axis, pairs)
        return values


def on_device(
    axes,
    tokens,
    cotangent,
    lengths,
    w_query,
    query_mean,
    query_square,
    w_keyval,
    keyval_mean,
    keyval_square,
    w_out,
    out_mean,
    out_square,
    w_gateup,
    gateup_mean,
    gateup_square,
    w_down,
    down_mean,
    down_square,
    norm_gains,
    norm_mean,
    norm_square,
    head_gains,
    head_mean,
    head_square,
):
    side = lax.axis_index("tensor")
    tok_rows = tokens.shape[0]
    cap = 2 * tok_rows
    length = lengths[0]
    order = Order(side, length, lax.axis_index(axes[2]) if len(axes) == 3 else jnp.zeros_like(side))
    summer = Summer(axes, order, side)

    def swap(piece):
        return lax.ppermute(piece, "tensor", [(0, 1), (1, 0)])

    def there(*arrays):
        return [v for v in arrays if v is not None]

    def gather(shard):
        return lax.all_gather(shard, axes, axis=0, tiled=True)

    shard = w_query.shape[0]
    heads = w_keyval.shape[2] // HD
    group = w_query.shape[1] // HD // heads
    units = w_gateup.shape[2]
    tiles = units // TILE
    part = tiles // CHUNKS
    kv_low = w_keyval.astype(BF).reshape(shard, 2, heads, HD)
    qkv_shard = jnp.concatenate(
        [w_query.astype(BF).reshape(shard, heads, group * HD), kv_low[:, 0], kv_low[:, 1]], axis=2
    ).reshape(shard, heads * (group + 2) * HD)
    out_shard = w_out.astype(BF).T
    pair_low = w_gateup.astype(BF).reshape(shard, 2, tiles, TILE)
    down_low = w_down.astype(BF).T.reshape(shard, tiles, TILE)
    pair_low = jnp.stack([pair_low[:, 0], pair_low[:, 1]], axis=2).reshape(shard, CHUNKS, part * PAIR)
    down_low = down_low.reshape(shard, CHUNKS, part * TILE)
    mlp_shard = jnp.concatenate([pair_low, down_low], axis=2).reshape(shard, tiles * WIDE)

    stream = tokens.astype(F32)
    normed_own = (stream * rms_parts(stream) * norm_gains[0]).astype(BF)
    normed_other = swap(normed_own)
    qkv_cols, out_cols = qkv_shard.shape[1], out_shard.shape[1]
    early = gather(jnp.concatenate([qkv_shard, out_shard], axis=1))
    most = gather(mlp_shard[:, : (CHUNKS - 1) * part * WIDE])
    late = gather(mlp_shard[:, (CHUNKS - 1) * part * WIDE :])
    parts = [(most, part * p) for p in range(CHUNKS - 1)] + [(late, 0)]

    own_places = side * tok_rows + jnp.arange(tok_rows)
    live = (own_places < length)[:, None]
    back_own = jnp.where(live, cotangent, jnp.zeros_like(cotangent))
    back_other = swap(back_own)
    cosine, sine = rope_tables(cap)

    def there(*arrays):
        return [v for v in arrays if v is not None]

    normed_cols = summer.columns(normed_own, normed_other, True)

    qkv, attended = attend(order, normed_own, normed_other, early, cosine, sine, head_gains, heads, group)
    attended_core = summer.other_core(attended)
    out_pair = [(attended, 0, early, qkv_cols // BLOCK)]
    attended_sent = swap(contract(order, OTHER_SIDE, out_pair, BF))
    back_cols = summer.columns(back_own, back_other, False)
    attended_here = contract(order, SIDE, out_pair, F32, after=there(normed_cols[1], attended_core))
    middle, second_own = middle_rows(order, tokens, attended_here, attended_sent, norm_gains)

    second = (second_own, swap(second_own))
    back = (back_own, back_other)
    pair_blocks, down_blocks = part * PAIR // BLOCK, part * TILE // BLOCK
    part_blocks = pair_blocks + down_blocks

    def mlp(weights, count, after=(), through=()):
        grads, hidden, *handed = swiglu(order, second, back, weights, count, part, after, through)
        return ((grads, summer.other_core(grads)), (hidden, summer.other_core(hidden))), *handed

    def mlp_items(p):
        (grads, hidden), first = mlp_pieces[p // (CHUNKS - 1)], parts[p][1]
        return [(second_cols, grads, PAIR, first, part), (back_cols, hidden, TILE, first, part)]

    def second_pairs(p):
        (grads, _), weights, at = mlp_pieces[p // (CHUNKS - 1)], parts[p][0], parts[p][1] // part
        return [(grads[0], at * pair_blocks + b, weights, at * part_blocks + b) for b in range(pair_blocks)]

    def down_pairs(p):
        (_, hidden), weights, at = mlp_pieces[p // (CHUNKS - 1)], parts[p][0], parts[p][1] // part
        first = at * part_blocks + pair_blocks
        return [(hidden[0], at * down_blocks + b, weights, first + b) for b in range(down_blocks)]

    all_down = lambda: [pair for p in range(CHUNKS) for pair in down_pairs(p)]

    out_rows = early.shape[0] // 2
    core = order.scalars[CORE]
    out_half = lax.dynamic_slice(early, (core * out_rows, qkv_cols), (out_rows, out_cols))

    second_cols = summer.columns(*second, False)
    first_piece, out_half = mlp(most, CHUNKS - 1, there(back_cols[1]), [out_half])
    out_got = swap(out_half)
    mlp_pieces = [first_piece]
    d_second_part = contract(order, SECOND, second_pairs(0) + second_pairs(1), BF, after=there(second_cols[1]))
    line_sum = summer.grad_by_line(mlp_items(0))
    mlp_grads = [summer.grad(mlp_items(1))]
    last_piece, out_got = mlp(late, 1, through=[out_got])
    mlp_pieces.append(last_piece)
    d_second_sent = swap(contract(order, SECOND, second_pairs(2), BF, [d_second_part]))
    if summer.lines:
        out_other = [(out_got, 0, CORE), (summer.other_core(out_got), 0, OTHER_CORE)]
    else:
        out_other = [(swap(early[:, qkv_cols:]), 0, FIRST)]
    mlp_grads.append(summer.grad(mlp_items(2)))
    d_second = contract(order, FIRST, [pair for p in range(CHUNKS) for pair in second_pairs(p)], F32)
    d_middle, branch_own, branch_again, g_second_gain = norm_back(
        order, 1, d_second, d_second_sent, middle, back_own, norm_gains, 2
    )

    there_a, there_b = project(order, branch_own, out_other, out_cols)
    sent_a, sent_b = swap(there_a), swap(there_b)
    mlp_sums = [summer.finish(mlp_grads[0], after=[line_sum])]
    here_a, here_b, branch_again = project(
        order, branch_own, [(early, qkv_cols // out_cols, FIRST)], out_cols, [branch_again]
    )
    branch_other = swap(branch_again)

    def attention_back(half, here, sent, after=(), through=()):
        span = (half * heads // 2, heads // 2)
        d_part, g_part, *handed = attend_back(
            order, qkv, here, sent, cosine, sine, head_gains, span, group, after, through
        )
        return d_part, summer.other_core(d_part), g_part[:2], *handed

    d_qkv_a, core_a, g_head_a = attention_back(0, here_a, sent_a)
    d_qkv_b, core_b, g_head_b = attention_back(1, here_b, sent_b)
    qkv_grads = [
        summer.grad([(normed_cols, (d_qkv_a, core_a), 512, 0, d_qkv_a.shape[1] // 512)]),
        summer.grad([(normed_cols, (d_qkv_b, core_b), 512, 0, d_qkv_b.shape[1] // 512)]),
    ]
    mlp_sums.append(summer.finish(mlp_grads[1], after=mlp_sums[-1:]))
    line_got = summer.trade_by_line(line_sum)
    out_here, out_there = contract_both(order, FIRST, all_down())
    out_sent = swap(out_there)
    branch_cols = summer.columns(branch_again, branch_other, True)
    qkv_pairs = [(d_qkv_a, 0, early, 0), (d_qkv_b, 0, early, 1)]
    d_first, d_first_there = contract_both(order, SIDE, qkv_pairs)
    d_first_sent = swap(d_first_there)
    mlp_sums.insert(0, summer.finish_by_line(line_sum, line_got))
    qkv_sum = summer.finish(*qkv_grads, after=mlp_sums[-1:])
    out_grad = summer.grad([(branch_cols, (attended, attended_core), 512, 0, out_cols // 512)])
    wide_rate = RATE_SCALE * D ** (-0.5)
    mlp_new = adam_mlp(
        order,
        (w_gateup, gateup_mean, gateup_square),
        (w_down, down_mean, down_square),
        mlp_sums,
        (wide_rate, RATE_SCALE * FF ** (-0.5)),
    )
    out_sum = summer.finish(out_grad)
    qkv_new = adam_qkv(
        order, (w_query, query_mean, query_square), (w_keyval, keyval_mean, keyval_square), qkv_sum, heads, wide_rate
    )
    order.rate = 0
    tokens_grad, g_first_gain = norm_back(order, 0, d_first, d_first_sent, tokens, d_middle, norm_gains, 0)
    layer_out = sum_rows(order, middle, out_here, out_sent)
    out_new = adam_out(order, (w_out, out_mean, out_square), out_sum, RATE_SCALE * OUT_FAN ** (-0.5))
    g_head = g_head_a + g_head_b

    gains_here = jnp.concatenate([g_first_gain[0], g_second_gain[0], g_head.reshape(-1)]).reshape(-1, HD)
    gain_sums = summer.everywhere(gains_here).reshape(-1)
    norm_sum = gain_sums[: 2 * D].reshape(2, D)
    head_sum = gain_sums[2 * D :].reshape(2, HD)

    norm_new = adam_step(norm_gains, norm_mean, norm_square, norm_sum, GAIN_RATE, 0.0)
    head_new = adam_step(head_gains, head_mean, head_square, head_sum, GAIN_RATE, 0.0)
    return (layer_out, tokens_grad, *qkv_new, *out_new, *mlp_new, *norm_new, *head_new)


def solution(mesh):
    count, sides = mesh.shape["dp"], mesh.shape["tensor"]
    if count == 16:
        axes = ("z", "y", "core")
        grid = Mesh(mesh.devices.reshape(4, 2, 2, sides), (*axes, "tensor"))
    else:
        axes, grid = ("dp",), mesh
    rows = P((*axes, "tensor"), None)
    in_out = [P(axes, "tensor")] * 3 + [P(axes, None, "tensor")] * 3 + [P("tensor", axes)] * 3
    in_out += [P(axes, None, "tensor")] * 3 + [P("tensor", axes)] * 3 + [P()] * 6
    return jax.shard_map(
        functools.partial(on_device, axes),
        mesh=grid,
        in_specs=(rows, rows, P(axes), *in_out),
        out_specs=(rows, rows, *in_out),
        check_vma=False,
    )
```

```python
import functools

import jax
import jax.numpy as jnp
from jax import lax
from jax.experimental import pallas as pl
from jax.experimental.pallas import tpu as pltpu
from jax.sharding import Mesh
from jax.sharding import PartitionSpec as P

D = 2048
HD = 128
FF = 6144
STEP = 10
LEN_MIN = 640

EPS_NORM = 1e-06
ROPE_BASE = 1000000.0
BETA_ONE = 0.9
BETA_TWO = 0.95
ADAM_EPS = 1e-08
WEIGHT_DECAY = 0.1
RATE_SCALE = 2.0
GAIN_RATE = 0.6
OUT_FAN = 8.0
LOG2_E = 1.4426950408889634

BF = jnp.bfloat16
F32 = jnp.float32
ROWS = 256
TILE = 256
BLOCK = 1024
CHUNKS = 3
WORK = 10**10

NN = (((1,), (0,)), ((), ()))
NT = (((1,), (1,)), ((), ()))
TN = (((0,), (0,)), ((), ()))


def mm(a, b, dims=NN):
    return lax.dot_general(a, b, dims, preferred_element_type=F32)


class Order:
    def __init__(self, side, length, core):
        self.rate = WORK
        one = jnp.ones_like(side)
        self.scalars = jnp.stack([side, 1 - side, length, 0 * one, one, core, 1 - core]).astype(jnp.int32)

    def call(self, kernel, grid, ins, outs, operands, *, after=(), through=(), vmem=48, scratch=(), work, name):
        count, later, made = len(ins), len(after) + len(through), len(outs)
        anywhere = pl.BlockSpec(memory_space=pl.ANY)

        def run(scalars, *refs):
            first = count + later
            token = refs[first + made]
            for i in range(token.shape[0]):
                token[i] = scalars[i]
            kernel(scalars, *refs[:count], *refs[first : first + made], *refs[first + made + 1 + len(through) :])

        results = pl.pallas_call(
            run,
            grid_spec=pltpu.PrefetchScalarGridSpec(
                num_scalar_prefetch=1,
                grid=grid,
                in_specs=[*ins, *[anywhere] * later],
                out_specs=[spec for spec, _ in outs] + [pl.BlockSpec(memory_space=pltpu.SMEM)] + [anywhere] * len(through),
                scratch_shapes=scratch,
            ),
            out_shape=[shape for _, shape in outs]
            + [shaped(self.scalars.shape, jnp.int32)]
            + [shaped(v.shape, v.dtype) for v in through],
            input_output_aliases={1 + count + len(after) + i: made + 1 + i for i in range(len(through))},
            compiler_params=pltpu.CompilerParams(vmem_limit_bytes=vmem * 2**20),
            cost_estimate=pl.CostEstimate(flops=int(work * self.rate) + 1, bytes_accessed=1, transcendentals=0),
            name=name,
        )(self.scalars, *operands, *after, *through)
        self.scalars = results[made]
        return results[:made] + results[made + 1 :]


SIDE, OTHER_SIDE, LENGTH, FIRST, SECOND, CORE, OTHER_CORE = range(7)


def shaped(shape, dtype):
    return jax.ShapeDtypeStruct(shape, dtype)


def held(shape):
    return pl.BlockSpec(shape, lambda *_: (0,) * len(shape), pipeline_mode=pl.Buffered(1))


def turn(values, gain, cosine, sine):
    scale = lax.rsqrt(jnp.mean(values * values, axis=-1, keepdims=True) + EPS_NORM)
    normed = values * scale * gain
    return normed * cosine + pltpu.roll(normed, HD // 2, 1) * sine


def turn_back(grad, values, gain, cosine, sine):
    scale = lax.rsqrt(jnp.mean(values * values, axis=-1, keepdims=True) + EPS_NORM)
    d_normed = grad * cosine + pltpu.roll(grad * sine, HD // 2, 1)
    hat = values * scale
    d_gain = jnp.sum(d_normed * hat, axis=0, keepdims=True)
    d_hat = d_normed * gain
    inner = jnp.mean(d_hat * hat, axis=-1, keepdims=True)
    return scale * (d_hat - hat * inner), d_gain


def key_spans(block):
    start = block * ROWS
    free = min(start, LEN_MIN // ROWS * ROWS)
    spans = []
    if free:
        spans.append((0, free, False, False))
    if start > free:
        spans.append((free, start, False, True))
    spans.append((start, start + ROWS, True, start + ROWS > LEN_MIN))
    return spans


def raised_scores(query, keys, span, length):
    first, last, causal, ragged = span
    scores = mm(query, keys[first:last], NT) * (HD**-0.5 * LOG2_E)
    raised = jnp.exp2(scores)
    allowed = None
    shape = raised.shape
    if causal:
        place = lax.broadcasted_iota(jnp.int32, shape, 0) % ROWS
        allowed = lax.broadcasted_iota(jnp.int32, shape, 1) <= place
    if ragged:
        live = lax.broadcasted_iota(jnp.int32, shape, 1) + first < length
        allowed = live if allowed is None else allowed & live
    return raised if allowed is None else jnp.where(allowed, raised, 0.0)


def split_heads(qkv_ref, group):
    width = group * HD
    queries = [qkv_ref[:, h * HD : (h + 1) * HD] for h in range(group)]
    return queries, qkv_ref[:, width : width + HD], qkv_ref[:, width + HD : width + 2 * HD]


def attend_kernel(group, place_ref, own_ref, other_ref, weight_ref, cos_ref, sin_ref, gain_ref, qkv_ref, out_ref):
    side, length = place_ref[SIDE], place_ref[LENGTH]
    half = own_ref.shape[0]
    qkv_ref[pl.ds(pl.multiple_of(side * half, half), half), :] = mm(own_ref[...], weight_ref[...])
    qkv_ref[pl.ds(pl.multiple_of((1 - side) * half, half), half), :] = mm(other_ref[...], weight_ref[...])
    cosine, sine = cos_ref[...], sin_ref[...]
    queries, keys, values = split_heads(qkv_ref, group)
    turned = [turn(q, gain_ref[0:1], cosine, sine).astype(BF) for q in queries]
    keys = turn(keys, gain_ref[1:2], cosine, sine).astype(BF)
    values = values.astype(BF)
    for block in range(qkv_ref.shape[0] // ROWS):
        rows = slice(block * ROWS, (block + 1) * ROWS)
        query = jnp.concatenate([t[rows] for t in turned], axis=0)
        total, mixed = 0.0, 0.0
        for span in key_spans(block):
            raised = raised_scores(query, keys, span, length)
            total = total + jnp.sum(raised, axis=-1, keepdims=True)
            mixed = mixed + mm(raised.astype(BF), values[span[0] : span[1]])
        mixed = (mixed / total).astype(BF)
        for h in range(group):
            out_ref[rows, h * HD : (h + 1) * HD] = mixed[h * ROWS : (h + 1) * ROWS]


def attend_back_kernel(
    group,
    place_ref,
    qkv_ref,
    own_ref,
    other_ref,
    cos_ref,
    sin_ref,
    gain_ref,
    out_ref,
    gain_out,
    grad_ref,
    dk_ref,
    dv_ref,
):
    side, length = place_ref[SIDE], place_ref[LENGTH]
    half = own_ref.shape[0]
    grad_ref[pl.ds(pl.multiple_of(side * half, half), half), :] = own_ref[...]
    grad_ref[pl.ds(pl.multiple_of((1 - side) * half, half), half), :] = other_ref[...]
    cosine, sine = cos_ref[...], sin_ref[...]
    queries, raw_keys, values = split_heads(qkv_ref, group)
    turned = [turn(q, gain_ref[0:1], cosine, sine).astype(BF) for q in queries]
    keys = turn(raw_keys, gain_ref[1:2], cosine, sine).astype(BF)
    values = values.astype(BF)
    dk_ref[...] = jnp.zeros_like(dk_ref)
    dv_ref[...] = jnp.zeros_like(dv_ref)
    q_gain = jnp.zeros((1, HD), F32)
    for block in range(qkv_ref.shape[0] // ROWS):
        rows = slice(block * ROWS, (block + 1) * ROWS)
        query = jnp.concatenate([t[rows] for t in turned], axis=0)
        grad = jnp.concatenate([grad_ref[rows, h * HD : (h + 1) * HD] for h in range(group)], axis=0)
        spans = key_spans(block)
        raised = [raised_scores(query, keys, span, length) for span in spans]
        total = sum(jnp.sum(r, axis=-1, keepdims=True) for r in raised)
        fix = 1.0 / total
        chances = [r * fix for r in raised]
        d_chances = [mm(grad, values[s[0] : s[1]], NT) for s in spans]
        inner = sum(jnp.sum(c * d, axis=-1, keepdims=True) for c, d in zip(chances, d_chances, strict=True))
        d_query = 0.0
        for span, chance, d_chance in zip(spans, chances, d_chances, strict=True):
            d_score = (chance * (d_chance - inner) * (HD**-0.5)).astype(BF)
            part = slice(span[0], span[1])
            d_query = d_query + mm(d_score, keys[part])
            dk_ref[part, :] += mm(d_score, query, TN)
            dv_ref[part, :] += mm(chance.astype(BF), grad, TN)
        for h in range(group):
            cols = slice(h * HD, (h + 1) * HD)
            d_raw, d_gain = turn_back(
                d_query[h * ROWS : (h + 1) * ROWS], qkv_ref[rows, cols], gain_ref[0:1], cosine[rows], sine[rows]
            )
            out_ref[rows, cols] = d_raw.astype(BF)
            q_gain = q_gain + d_gain
    width = group * HD
    d_raw, k_gain = turn_back(dk_ref[...], raw_keys, gain_ref[1:2], cosine, sine)
    out_ref[:, width : width + HD] = d_raw.astype(BF)
    out_ref[:, width + HD : width + 2 * HD] = dv_ref[...].astype(BF)

    @pl.when(pl.program_id(0) == 0)
    def _():
        gain_out[...] = jnp.zeros_like(gain_out)

    gain_out[0:1, :] += q_gain
    gain_out[1:2, :] += k_gain


def attend(order, own, other, weights, cosine, sine, gains, heads, group):
    half, width = own.shape
    cap, cols = 2 * half, (group + 2) * HD
    return order.call(
        functools.partial(attend_kernel, group),
        (heads,),
        [
            held((half, width)),
            held((half, width)),
            pl.BlockSpec((width, cols), lambda n, s: (0, n)),
            held((cap, HD)),
            held((cap, HD)),
            held((2, HD)),
        ],
        [
            (pl.BlockSpec((cap, cols), lambda n, s: (0, n)), shaped((cap, heads * cols), F32)),
            (pl.BlockSpec((cap, group * HD), lambda n, s: (0, n)), shaped((cap, heads * group * HD), BF)),
        ],
        (own, other, weights, cosine, sine, gains),
        work=24,
        name="attend",
    )


def attend_back(order, qkv, own, other, cosine, sine, gains, span, group, after=(), through=()):
    half, cap, cols = own.shape[0], 2 * own.shape[0], (group + 2) * HD
    first, heads = span
    rows = pl.BlockSpec((half, group * HD), lambda n, s: (0, n))
    return order.call(
        functools.partial(attend_back_kernel, group),
        (heads,),
        [
            pl.BlockSpec((cap, cols), lambda n, s: (0, first + n)),
            rows,
            rows,
            held((cap, HD)),
            held((cap, HD)),
            held((2, HD)),
        ],
        [
            (pl.BlockSpec((cap, cols), lambda n, s: (0, n)), shaped((cap, heads * cols), BF)),
            (pl.BlockSpec((8, HD), lambda n, s: (0, 0)), shaped((8, HD), F32)),
        ],
        (qkv, own, other, cosine, sine, gains),
        after=after,
        through=through,
        scratch=[pltpu.VMEM((cap, group * HD), BF), pltpu.VMEM((cap, HD), F32), pltpu.VMEM((cap, HD), F32)],
        work=17,
        name="attend_back",
    )


def project_kernel(count, place_ref, *refs):
    for out_ref, at in ((refs[-2], 0), (refs[-1], refs[-2].shape[1])):
        cols = slice(at, at + out_ref.shape[1])
        out_ref[...] = sum(mm(refs[i][...], refs[count + i][:, cols]) for i in range(count)).astype(BF)


def project(order, rows, weights, cols, through=()):
    half, depth = rows.shape[0], weights[0][0].shape[0]
    left = [pl.BlockSpec((half, depth), functools.partial(lambda at, j, s: (0, s[at]), at)) for _, _, at in weights]
    right = [pl.BlockSpec((depth, cols), functools.partial(lambda at, j, s: (0, at), at)) for _, at, _ in weights]
    out = pl.BlockSpec((half, cols // 2), lambda j, s: (0, 0))
    return order.call(
        functools.partial(project_kernel, len(weights)),
        (1,),
        left + right,
        [(out, shaped((half, cols // 2), BF))] * 2,
        (*[rows] * len(weights), *[w for w, _, _ in weights]),
        through=through,
        work=5,
        name="project",
    )


WIDE = 3 * TILE
PAIR = 2 * TILE


def swiglu_kernel(place_ref, second_own, second_other, back_own, back_other, pair_ref, down_ref, grad_ref, hidden_ref):
    half = second_own.shape[0]
    for at, second_ref, back_ref in ((0, second_own, back_own), (half, second_other, back_other)):
        rows = slice(at, at + half)
        pair = mm(second_ref[...], pair_ref[...])
        d_hidden = mm(back_ref[...], down_ref[...])
        gate, up = pair[:, :TILE], pair[:, TILE:]
        sigmoid = 1.0 / (1.0 + jnp.exp(-gate))
        silu = gate * sigmoid
        d_gate = d_hidden * up * (sigmoid * (1.0 + gate * (1.0 - sigmoid)))
        grad_ref[rows, :TILE] = d_gate.astype(BF)
        grad_ref[rows, TILE:] = (d_hidden * silu).astype(BF)
        hidden_ref[rows, :] = (silu * up).astype(BF)


def swiglu(order, second, back, weights, count, tiles, after=(), through=()):
    half, width = second[0].shape
    rows = held((half, width))
    pair_at = lambda j: j // tiles * (3 * tiles // 2) + j % tiles
    down_at = lambda j: j // tiles * (3 * tiles) + 2 * tiles + j % tiles
    return order.call(
        swiglu_kernel,
        (count * tiles,),
        [
            rows,
            rows,
            rows,
            rows,
            pl.BlockSpec((width, PAIR), lambda j, s: (0, pair_at(j))),
            pl.BlockSpec((width, TILE), lambda j, s: (0, down_at(j))),
        ],
        [
            (pl.BlockSpec((2 * half, PAIR), lambda j, s: (0, j)), shaped((2 * half, count * tiles * PAIR), BF)),
            (pl.BlockSpec((2 * half, TILE), lambda j, s: (0, j)), shaped((2 * half, count * tiles * TILE), BF)),
        ],
        (*second, *back, weights, weights),
        after=after,
        through=through,
        work=5 * count * tiles,
        name="swiglu",
    )


def turn_columns_kernel(which, place_ref, own_keep, other_keep, own_send, other_send, keep_ref, send_ref):
    half = own_keep.shape[0]
    if which is None:
        own_at, other_at = slice(0, half), slice(half, 2 * half)
    else:
        own_at = pl.ds(pl.multiple_of(place_ref[which] * half, half), half)
        other_at = pl.ds(pl.multiple_of((1 - place_ref[which]) * half, half), half)
    keep_ref[:, own_at] = own_keep[...].T
    keep_ref[:, other_at] = other_keep[...].T
    send_ref[:, own_at] = own_send[...].T
    send_ref[:, other_at] = other_send[...].T


def turn_columns(order, own, other, which, axes, after=()):
    half = own.shape[0]
    owned = own.shape[1] // 16
    y, c = lax.axis_index(axes[1]), lax.axis_index(axes[2])
    at = lambda j, mine: (j % 4) * 4 + jnp.where(j < 4, 1 - y, y) * 2 + jnp.where(mine, c, 1 - c)
    lines = jnp.arange(8, dtype=jnp.int32)
    table = jnp.concatenate([at(lines, True), at(lines, False)]).astype(jnp.int32)
    scalars = jnp.concatenate([order.scalars, table])
    base = order.scalars.shape[0]
    keep = pl.BlockSpec((half, owned), lambda j, s: (0, s[base + j]))
    send = pl.BlockSpec((half, owned), lambda j, s: (0, s[base + 8 + j]))
    out = pl.BlockSpec((owned, 2 * half), lambda j, s: (j, 0))
    held_back, order.scalars = order.scalars, scalars
    keep_cols, send_cols = order.call(
        functools.partial(turn_columns_kernel, which),
        (8,),
        [keep, keep, send, send],
        [(out, shaped((8 * owned, 2 * half), BF))] * 2,
        (own, other, own, other),
        after=after,
        work=7,
        name="turn_columns",
    )
    order.scalars = order.scalars[:base]
    return keep_cols, send_cols


def weight_grad_kernel(widths, place_ref, *refs):
    outs = refs[4 * len(widths) :]
    half = refs[0].shape[0] // 2
    first = 0
    for i, width in enumerate(widths):
        left, far_left, right, far_right = refs[4 * i : 4 * i + 4]
        cols = slice(first, first + width)
        first += width
        product = mm(left[...], right[...]) + mm(far_left[...], far_right[...])
        if len(outs) == 2:
            outs[0][:, cols] = product[:half].astype(BF)
            outs[1][:, cols] = product[half:].astype(BF)
            continue
        for line in range(4):
            at, owned = line * half // 2, half // 4
            outs[0][at : at + owned, cols] = product[line * owned : (line + 1) * owned].astype(BF)
            outs[0][at + owned : at + 2 * owned, cols] = product[half + line * owned : half + (line + 1) * owned].astype(BF)


def weight_grad(order, items, by_line=False, after=()):
    rows, cap = items[0][0][0].shape
    widths = [width for _, _, width, _, _ in items]
    steps, step = items[0][4], sum(widths)
    out_rows = rows if by_line else rows // 2
    out = (pl.BlockSpec((out_rows, step), lambda j, s: (0, j)), shaped((out_rows, steps * step), BF))
    ins = []
    for _, _, width, first, _ in items:
        ins += [held((rows, cap))] * 2
        ins += [pl.BlockSpec((cap, width), functools.partial(lambda first, j, s: (0, first + j), first))] * 2
    return order.call(
        functools.partial(weight_grad_kernel, widths),
        (steps,),
        ins,
        [out] if by_line else [out, out],
        [part for left, right, *_ in items for part in (*left, *right)],
        after=after,
        work=steps * step // 160,
        name="weight_grad",
    )


def contract_kernel(count, adds, place_ref, *refs):
    total = 0.0
    for i in range(count):
        total = total + mm(refs[i][...], refs[count + i][...], NT)
    for i in range(adds):
        total = total + refs[2 * count + i][...].astype(F32)
    refs[-1][...] = total.astype(refs[-1].dtype)


def contract(order, which, pairs, dtype, adds=(), after=()):
    half, width = pairs[0][0].shape[0] // 2, pairs[0][2].shape[0]
    step = 512
    ins = [
        pl.BlockSpec((half, BLOCK), functools.partial(lambda at, j, s: (s[which], at), at), pipeline_mode=pl.Buffered(1))
        for _, at, _, _ in pairs
    ]
    ins += [pl.BlockSpec((step, BLOCK), functools.partial(lambda at, j, s: (j, at), at)) for _, _, _, at in pairs]
    across = pl.BlockSpec((half, step), lambda j, s: (0, j))
    return order.call(
        functools.partial(contract_kernel, len(pairs), len(adds)),
        (width // step,),
        ins + [across] * len(adds),
        [(across, shaped((half, width), dtype))],
        (*[left for left, _, _, _ in pairs], *[weights for _, _, weights, _ in pairs], *adds),
        after=after,
        work=8 * len(pairs),
        name="contract",
    )[0]


def contract_both_kernel(which, count, place_ref, *refs):
    total = 0.0
    for i in range(count):
        total = total + mm(refs[i][...], refs[count + i][...], NT)
    half = total.shape[0] // 2
    first, second = total[:half], total[half:]
    here_ref, there_ref = refs[-2:]
    if which == FIRST:
        here_ref[...], there_ref[...] = first, second.astype(BF)
        return
    here = place_ref[which] == 0
    here_ref[...] = jnp.where(here, first, second)
    there_ref[...] = jnp.where(here, second, first).astype(BF)


def contract_both(order, which, pairs):
    rows, width = pairs[0][0].shape[0], pairs[0][2].shape[0]
    step = 512
    ins = [
        pl.BlockSpec((rows, BLOCK), functools.partial(lambda at, j, s: (0, at), at), pipeline_mode=pl.Buffered(1))
        for _, at, _, _ in pairs
    ]
    ins += [pl.BlockSpec((step, BLOCK), functools.partial(lambda at, j, s: (j, at), at)) for _, _, _, at in pairs]
    across = pl.BlockSpec((rows // 2, step), lambda j, s: (0, j))
    return order.call(
        functools.partial(contract_both_kernel, which, len(pairs)),
        (width // step,),
        ins,
        [(across, shaped((rows // 2, width), F32)), (across, shaped((rows // 2, width), BF))],
        (*[left for left, _, _, _ in pairs], *[weights for _, _, weights, _ in pairs]),
        work=5 * len(pairs),
        name="contract_both",
    )


LINES = 128


def lines_spec(width):
    return pl.BlockSpec((LINES, width), lambda j, s: (j, 0))


def middle_kernel(place_ref, tokens_ref, own_ref, sent_ref, gain_ref, middle_ref, second_ref):
    middle = tokens_ref[...].astype(F32) + own_ref[...] + sent_ref[...].astype(F32)
    middle_ref[...] = middle
    second_ref[...] = (middle * rms_parts(middle) * gain_ref[1:2, :]).astype(BF)


def middle_rows(order, tokens, own, sent, gains, after=()):
    rows, width = tokens.shape
    spec = lines_spec(width)
    return order.call(
        middle_kernel,
        (rows // LINES,),
        [spec, spec, spec, held((2, width))],
        [(spec, shaped((rows, width), F32)), (spec, shaped((rows, width), BF))],
        (tokens, own, sent, gains),
        after=after,
        work=6,
        name="middle_rows",
    )


def norm_back_kernel(which, place_ref, own_ref, sent_ref, value_ref, extra_ref, gain_ref, *outs):
    grad = own_ref[...] + sent_ref[...].astype(F32)
    values = value_ref[...].astype(F32)
    scale = rms_parts(values)
    hat = values * scale
    d_hat = grad * gain_ref[which : which + 1, :]
    inner = jnp.mean(d_hat * hat, axis=-1, keepdims=True)
    total = extra_ref[...].astype(F32) + scale * (d_hat - hat * inner)
    outs[0][...] = total
    for out in outs[1:-1]:
        out[...] = total.astype(BF)

    @pl.when(pl.program_id(0) == 0)
    def _():
        outs[-1][...] = jnp.zeros_like(outs[-1])

    outs[-1][0:1, :] += jnp.sum(grad * hat, axis=0, keepdims=True)


def norm_back(order, which, own, sent, values, extra, gains, low):
    rows, width = own.shape
    spec = lines_spec(width)
    outs = [(spec, shaped((rows, width), F32))]
    outs += [(spec, shaped((rows, width), BF))] * low
    outs.append((pl.BlockSpec((8, width), lambda j, s: (0, 0)), shaped((8, width), F32)))
    return order.call(
        functools.partial(norm_back_kernel, which),
        (rows // LINES,),
        [spec, spec, spec, spec, held((2, width))],
        outs,
        (own, sent, values, extra, gains),
        work=8,
        name="norm_back",
    )


def sum_kernel(place_ref, *refs):
    refs[-1][...] = sum(r[...].astype(F32) for r in refs[:-1])


def sum_rows(order, *arrays):
    rows, width = arrays[0].shape
    spec = lines_spec(width)
    out = (spec, shaped((rows, width), F32))
    return order.call(sum_kernel, (rows // LINES,), [spec] * len(arrays), [out], arrays, work=4, name="sum_rows")[0]


def add_kernel(place_ref, *refs):
    at = 0
    for i in range(len(refs) // 2):
        a, b = refs[2 * i], refs[2 * i + 1]
        refs[-1][:, at : at + a.shape[1]] = (a[...].astype(F32) + b[...].astype(F32)).astype(BF)
        at += a.shape[1]


def add_pairs(order, pairs, skip=0, after=()):
    rows = pairs[0][1].shape[0]
    lines = min(LINES, rows)
    flat = [part for pair in pairs for part in pair]
    width = sum(a.shape[1] for a, _ in pairs)
    spec = lambda width, skip: pl.BlockSpec((lines, width), lambda j, s: (j + skip, 0))
    return order.call(
        add_kernel,
        (rows // lines,),
        [spec(a.shape[1], skip * (i == 0)) for pair in pairs for i, a in enumerate(pair)],
        [(spec(width, 0), shaped((rows, width), BF))],
        flat,
        after=after,
        work=5,
        vmem=62, name="add_pairs",
    )[0]


def take_kernel(place_ref, from_ref, out_ref):
    out_ref[...] = from_ref[...]


def take_rows(order, array):
    rows, width = array.shape
    block = pl.BlockSpec((rows // 2, width), lambda j, s: (0, 0))
    return order.call(
        take_kernel, (1,), [block], [(block, shaped((rows // 2, width), array.dtype))], [array], work=2, vmem=62, name="take_rows"
    )[0]


def adam_qkv_kernel(rate, place_ref, *refs):
    query, keyval, sums, query_out, keyval_out = refs[0:3], refs[3:6], refs[6], refs[7:10], refs[10:13]
    width = query[0].shape[1]
    new = adam_step(*[r[...] for r in query], sums[:, :width].astype(F32), rate, WEIGHT_DECAY)
    for out, value in zip(query_out, new, strict=True):
        out[...] = value
    for i in range(2):
        grad = sums[:, width + i * HD : width + (i + 1) * HD].astype(F32)
        new = adam_step(*[r[:, i, :] for r in keyval], grad, rate, WEIGHT_DECAY)
        for out, value in zip(keyval_out, new, strict=True):
            out[:, i, :] = value


def adam_qkv(order, query, keyval, sums, heads, rate):
    shard, wide = query[0].shape
    queries = pl.BlockSpec((shard, wide // heads), lambda j, s: (0, j))
    pair = pl.BlockSpec((shard, 2, HD), lambda j, s: (0, 0, j))
    return order.call(
        functools.partial(adam_qkv_kernel, rate),
        (heads,),
        [queries] * 3 + [pair] * 3 + [pl.BlockSpec((shard, wide // heads + 2 * HD), lambda j, s: (0, j))],
        [(queries, shaped(query[0].shape, F32))] * 3 + [(pair, shaped(keyval[0].shape, F32))] * 3,
        (*query, *keyval, sums),
        work=5,
        vmem=62, name="adam_qkv",
    )


def adam_out_kernel(rate, place_ref, *refs):
    new = adam_step(*[r[...] for r in refs[0:3]], refs[3][...].astype(F32).T, rate, WEIGHT_DECAY)
    for out, value in zip(refs[4:7], new, strict=True):
        out[...] = value


def adam_out(order, weights, sums, rate):
    tall, shard = weights[0].shape
    block = pl.BlockSpec((256, shard), lambda j, s: (j, 0))
    return order.call(
        functools.partial(adam_out_kernel, rate),
        (tall // 256,),
        [block] * 3 + [pl.BlockSpec((shard, 256), lambda j, s: (0, j))],
        [(block, shaped(weights[0].shape, F32))] * 3,
        (*weights, sums),
        work=3,
        vmem=62, name="adam_out",
    )


def adam_kernel(rates, place_ref, *refs):
    pair, down, all_sums, (pair_out, down_out), grad_ref = refs[0:3], refs[3:6], refs[6:-7], (refs[-7:-4], refs[-4:-1]), refs[-1]
    at = pl.program_id(0) // (pl.num_programs(0) // len(all_sums))
    sums = all_sums[0][...]
    for i in range(1, len(all_sums)):
        sums = jnp.where(at == i, all_sums[i][...], sums)
    sums = sums.astype(F32)
    down_grads = []
    for tile in range(2):
        first = tile * WIDE
        for piece in range(TILE // HD):
            for i in range(2):
                cols = slice(first + i * TILE + piece * HD, first + i * TILE + (piece + 1) * HD)
                grad_ref[:, tile * 4 + piece * 2 + i, :] = sums[:, cols]
        down_grads.append(sums[:, first + PAIR : first + WIDE].T)
    new = adam_step(*[r[...] for r in pair], grad_ref[...], rates[0], WEIGHT_DECAY)
    for out, value in zip(pair_out, new, strict=True):
        out[...] = value
    new = adam_step(*[r[...] for r in down], jnp.concatenate(down_grads, axis=0), rates[1], WEIGHT_DECAY)
    for out, value in zip(down_out, new, strict=True):
        out[...] = value


def adam_mlp(order, pair, down, sums, rates):
    shard, _, units = pair[0].shape
    rows = units // HD * 2
    seen = [v.reshape(shard, 2, units // HD, HD).transpose(0, 2, 1, 3).reshape(shard, rows, HD) for v in pair]
    wide = pl.BlockSpec((shard, 8, HD), lambda j, s: (0, j, 0))
    tall = pl.BlockSpec((2 * TILE, shard), lambda j, s: (j, 0))
    steps = units // TILE // len(sums) // 2
    part = lambda i: pl.BlockSpec((shard, 2 * WIDE), lambda j, s: (0, jnp.clip(j - i * steps, 0, steps - 1)))
    new = order.call(
        functools.partial(adam_kernel, rates),
        (units // TILE // 2,),
        [wide] * 3 + [tall] * 3 + [part(i) for i in range(len(sums))],
        [(wide, shaped(seen[0].shape, F32))] * 3 + [(tall, shaped(down[0].shape, F32))] * 3,
        (*seen, *down, *sums),
        scratch=[pltpu.VMEM((shard, 8, HD), F32)],
        work=20,
        name="adam_mlp",
    )
    back = lambda v: v.reshape(shard, units // HD, 2, HD).transpose(0, 2, 1, 3).reshape(shard, 2, units)
    return [*[back(v) for v in new[:3]], *new[3:]]


def rms_parts(values):
    return lax.rsqrt(jnp.mean(values * values, axis=-1, keepdims=True) + EPS_NORM)


def rope_tables(row_count):
    places = jnp.arange(row_count).astype(F32)
    inverse_freq = ROPE_BASE ** (-(jnp.arange(HD // 2).astype(F32) * 2.0) / HD)
    angles = places[:, None] * inverse_freq[None, :]
    sine = jnp.sin(angles)
    cosine = jnp.cos(angles)
    return jnp.concatenate([cosine, cosine], axis=1), jnp.concatenate([-sine, sine], axis=1)


def adam_step(weight, mean_old, square, gradient, step_rate, decay_rate):
    new_mean = BETA_ONE * mean_old + (1.0 - BETA_ONE) * gradient
    new_square = BETA_TWO * square + (1.0 - BETA_TWO) * gradient * gradient
    fix_one = 1.0 - BETA_ONE**STEP
    fix_two = 1.0 - BETA_TWO**STEP
    update = new_mean / fix_one / (jnp.sqrt(new_square / fix_two) + ADAM_EPS)
    return (weight - step_rate * (update + decay_rate * weight), new_mean, new_square)


class Summer:
    def __init__(self, axes, order, side):
        self.axes, self.order, self.side = axes, order, side
        self.lines = len(axes) == 3

    def other_core(self, piece):
        return lax.ppermute(piece, self.axes[2], [(0, 1), (1, 0)]) if self.lines else None

    def columns(self, own, other, in_order, after=()):
        if not self.lines:
            if not in_order:
                return jnp.concatenate([own, other], axis=0)
            first = self.side == 0
            return jnp.concatenate([jnp.where(first, own, other), jnp.where(first, other, own)], axis=0)
        keep, send = turn_columns(self.order, own, other, SIDE if in_order else None, self.axes, after)
        return keep, self.other_core(send)

    def whole(self, items):
        parts = []
        for left, (right, _), width, first, steps in items:
            right = right[:, first * width : (first + steps) * width]
            parts.append(mm(left, right, TN).astype(BF).reshape(left.shape[1], -1, width))
        return jnp.concatenate(parts, axis=2).reshape(parts[0].shape[0], -1)

    def grad(self, items, after=()):
        if not self.lines:
            return (self.whole(items),)
        near, keep = weight_grad(self.order, items, after=after)
        return keep, lax.ppermute(near, self.axes[1], [(0, 1), (1, 0)])

    def grad_by_line(self, items, after=()):
        if not self.lines:
            return self.finish((self.whole(items),))
        (whole,) = weight_grad(self.order, items, True, after)
        return lax.psum_scatter(whole, self.axes[0], scatter_dimension=0, tiled=True)

    def trade_by_line(self, summed):
        if not self.lines:
            return None
        return lax.ppermute(take_rows(self.order, summed), self.axes[1], [(0, 1), (1, 0)])

    def finish_by_line(self, summed, got):
        return add_pairs(self.order, [(summed, got)], 1) if self.lines else summed

    def finish(self, *grads, after=()):
        if not self.lines:
            return lax.psum_scatter(jnp.concatenate([g for g, in grads], axis=1), self.axes, scatter_dimension=0, tiled=True)
        line = add_pairs(self.order, grads, after=after)
        return lax.psum_scatter(line, self.axes[0], scatter_dimension=0, tiled=True)

    def everywhere(self, values):
        if not self.lines:
            return lax.psum(values, (*self.axes, "tensor"))
        pair = [(0, 1), (1, 0)]
        steps = [(self.axes[2], pair), (self.axes[1], pair)]
        steps += [(self.axes[0], [(0, 1), (1, 0), (2, 3), (3, 2)]), (self.axes[0], [(0, 2), (2, 0), (1, 3), (3, 1)])]
        for axis, pairs in (*steps, ("tensor", pair)):
            values = values + lax.ppermute(values, axis, pairs)
        return values


def on_device(
    axes,
    tokens,
    cotangent,
    lengths,
    w_query,
    query_mean,
    query_square,
    w_keyval,
    keyval_mean,
    keyval_square,
    w_out,
    out_mean,
    out_square,
    w_gateup,
    gateup_mean,
    gateup_square,
    w_down,
    down_mean,
    down_square,
    norm_gains,
    norm_mean,
    norm_square,
    head_gains,
    head_mean,
    head_square,
):
    side = lax.axis_index("tensor")
    tok_rows = tokens.shape[0]
    cap = 2 * tok_rows
    length = lengths[0]
    order = Order(side, length, lax.axis_index(axes[2]) if len(axes) == 3 else jnp.zeros_like(side))
    summer = Summer(axes, order, side)

    def swap(piece):
        return lax.ppermute(piece, "tensor", [(0, 1), (1, 0)])

    def there(*arrays):
        return [v for v in arrays if v is not None]

    def gather(shard):
        return lax.all_gather(shard, axes, axis=0, tiled=True)

    shard = w_query.shape[0]
    heads = w_keyval.shape[2] // HD
    group = w_query.shape[1] // HD // heads
    units = w_gateup.shape[2]
    tiles = units // TILE
    part = tiles // CHUNKS
    kv_low = w_keyval.astype(BF).reshape(shard, 2, heads, HD)
    qkv_shard = jnp.concatenate(
        [w_query.astype(BF).reshape(shard, heads, group * HD), kv_low[:, 0], kv_low[:, 1]], axis=2
    ).reshape(shard, heads * (group + 2) * HD)
    out_shard = w_out.astype(BF).T
    pair_low = w_gateup.astype(BF).reshape(shard, 2, tiles, TILE)
    down_low = w_down.astype(BF).T.reshape(shard, tiles, TILE)
    pair_low = jnp.stack([pair_low[:, 0], pair_low[:, 1]], axis=2).reshape(shard, CHUNKS, part * PAIR)
    down_low = down_low.reshape(shard, CHUNKS, part * TILE)
    mlp_shard = jnp.concatenate([pair_low, down_low], axis=2).reshape(shard, tiles * WIDE)

    stream = tokens.astype(F32)
    normed_own = (stream * rms_parts(stream) * norm_gains[0]).astype(BF)
    normed_other = swap(normed_own)
    qkv_cols, out_cols = qkv_shard.shape[1], out_shard.shape[1]
    early = gather(jnp.concatenate([qkv_shard, out_shard], axis=1))
    most = gather(mlp_shard[:, : (CHUNKS - 1) * part * WIDE])
    late = gather(mlp_shard[:, (CHUNKS - 1) * part * WIDE :])
    parts = [(most, part * p) for p in range(CHUNKS - 1)] + [(late, 0)]

    own_places = side * tok_rows + jnp.arange(tok_rows)
    live = (own_places < length)[:, None]
    back_own = jnp.where(live, cotangent, jnp.zeros_like(cotangent))
    back_other = swap(back_own)
    cosine, sine = rope_tables(cap)

    def there(*arrays):
        return [v for v in arrays if v is not None]

    normed_cols = summer.columns(normed_own, normed_other, True)

    qkv, attended = attend(order, normed_own, normed_other, early, cosine, sine, head_gains, heads, group)
    attended_core = summer.other_core(attended)
    out_pair = [(attended, 0, early, qkv_cols // BLOCK)]
    attended_sent = swap(contract(order, OTHER_SIDE, out_pair, BF))
    back_cols = summer.columns(back_own, back_other, False)
    attended_here = contract(order, SIDE, out_pair, F32, after=there(normed_cols[1], attended_core))
    middle, second_own = middle_rows(order, tokens, attended_here, attended_sent, norm_gains)

    second = (second_own, swap(second_own))
    back = (back_own, back_other)
    pair_blocks, down_blocks = part * PAIR // BLOCK, part * TILE // BLOCK
    part_blocks = pair_blocks + down_blocks

    def mlp(weights, count, after=(), through=()):
        grads, hidden, *handed = swiglu(order, second, back, weights, count, part, after, through)
        return ((grads, summer.other_core(grads)), (hidden, summer.other_core(hidden))), *handed

    def mlp_items(p):
        (grads, hidden), first = mlp_pieces[p // (CHUNKS - 1)], parts[p][1]
        return [(second_cols, grads, PAIR, first, part), (back_cols, hidden, TILE, first, part)]

    def second_pairs(p):
        (grads, _), weights, at = mlp_pieces[p // (CHUNKS - 1)], parts[p][0], parts[p][1] // part
        return [(grads[0], at * pair_blocks + b, weights, at * part_blocks + b) for b in range(pair_blocks)]

    def down_pairs(p):
        (_, hidden), weights, at = mlp_pieces[p // (CHUNKS - 1)], parts[p][0], parts[p][1] // part
        first = at * part_blocks + pair_blocks
        return [(hidden[0], at * down_blocks + b, weights, first + b) for b in range(down_blocks)]

    all_down = lambda: [pair for p in range(CHUNKS) for pair in down_pairs(p)]

    out_rows = early.shape[0] // 2
    core = order.scalars[CORE]
    out_half = lax.dynamic_slice(early, (core * out_rows, qkv_cols), (out_rows, out_cols))

    second_cols = summer.columns(*second, False)
    first_piece, out_half = mlp(most, CHUNKS - 1, there(back_cols[1]), [out_half])
    out_got = swap(out_half)
    mlp_pieces = [first_piece]
    d_second_part = contract(order, SECOND, second_pairs(0) + second_pairs(1), BF, after=there(second_cols[1]))
    line_sum = summer.grad_by_line(mlp_items(0))
    mlp_grads = [summer.grad(mlp_items(1))]
    last_piece, out_got = mlp(late, 1, through=[out_got])
    mlp_pieces.append(last_piece)
    d_second_sent = swap(contract(order, SECOND, second_pairs(2), BF, [d_second_part]))
    if summer.lines:
        out_other = [(out_got, 0, CORE), (summer.other_core(out_got), 0, OTHER_CORE)]
    else:
        out_other = [(swap(early[:, qkv_cols:]), 0, FIRST)]
    mlp_grads.append(summer.grad(mlp_items(2)))
    d_second = contract(order, FIRST, [pair for p in range(CHUNKS) for pair in second_pairs(p)], F32)
    d_middle, branch_own, branch_again, g_second_gain = norm_back(
        order, 1, d_second, d_second_sent, middle, back_own, norm_gains, 2
    )

    there_a, there_b = project(order, branch_own, out_other, out_cols)
    sent_a, sent_b = swap(there_a), swap(there_b)
    here_a, here_b, branch_again = project(
        order, branch_own, [(early, qkv_cols // out_cols, FIRST)], out_cols, [branch_again]
    )
    branch_other = swap(branch_again)
    mlp_sums = [summer.finish(mlp_grads[0], after=[line_sum])]

    def attention_back(half, here, sent, after=(), through=()):
        span = (half * heads // 2, heads // 2)
        d_part, g_part, *handed = attend_back(
            order, qkv, here, sent, cosine, sine, head_gains, span, group, after, through
        )
        return d_part, summer.other_core(d_part), g_part[:2], *handed

    d_qkv_a, core_a, g_head_a = attention_back(0, here_a, sent_a)
    d_qkv_b, core_b, g_head_b = attention_back(1, here_b, sent_b)
    qkv_grads = [
        summer.grad([(normed_cols, (d_qkv_a, core_a), 512, 0, d_qkv_a.shape[1] // 512)]),
        summer.grad([(normed_cols, (d_qkv_b, core_b), 512, 0, d_qkv_b.shape[1] // 512)]),
    ]
    mlp_sums.append(summer.finish(mlp_grads[1], after=mlp_sums[-1:]))
    line_got = summer.trade_by_line(line_sum)
    out_here, out_there = contract_both(order, FIRST, all_down())
    out_sent = swap(out_there)
    branch_cols = summer.columns(branch_again, branch_other, True)
    qkv_pairs = [(d_qkv_a, 0, early, 0), (d_qkv_b, 0, early, 1)]
    d_first, d_first_there = contract_both(order, SIDE, qkv_pairs)
    d_first_sent = swap(d_first_there)
    mlp_sums.insert(0, summer.finish_by_line(line_sum, line_got))
    qkv_sum = summer.finish(*qkv_grads, after=mlp_sums[-1:])
    out_grad = summer.grad([(branch_cols, (attended, attended_core), 512, 0, out_cols // 512)])
    wide_rate = RATE_SCALE * D ** (-0.5)
    mlp_new = adam_mlp(
        order,
        (w_gateup, gateup_mean, gateup_square),
        (w_down, down_mean, down_square),
        mlp_sums,
        (wide_rate, RATE_SCALE * FF ** (-0.5)),
    )
    out_sum = summer.finish(out_grad)
    qkv_new = adam_qkv(
        order, (w_query, query_mean, query_square), (w_keyval, keyval_mean, keyval_square), qkv_sum, heads, wide_rate
    )
    order.rate = 0
    tokens_grad, g_first_gain = norm_back(order, 0, d_first, d_first_sent, tokens, d_middle, norm_gains, 0)
    layer_out = sum_rows(order, middle, out_here, out_sent)
    out_new = adam_out(order, (w_out, out_mean, out_square), out_sum, RATE_SCALE * OUT_FAN ** (-0.5))
    g_head = g_head_a + g_head_b

    gains_here = jnp.concatenate([g_first_gain[0], g_second_gain[0], g_head.reshape(-1)]).reshape(-1, HD)
    gain_sums = summer.everywhere(gains_here).reshape(-1)
    norm_sum = gain_sums[: 2 * D].reshape(2, D)
    head_sum = gain_sums[2 * D :].reshape(2, HD)

    norm_new = adam_step(norm_gains, norm_mean, norm_square, norm_sum, GAIN_RATE, 0.0)
    head_new = adam_step(head_gains, head_mean, head_square, head_sum, GAIN_RATE, 0.0)
    return (layer_out, tokens_grad, *qkv_new, *out_new, *mlp_new, *norm_new, *head_new)


def solution(mesh):
    count, sides = mesh.shape["dp"], mesh.shape["tensor"]
    if count == 16:
        axes = ("z", "y", "core")
        grid = Mesh(mesh.devices.reshape(4, 2, 2, sides), (*axes, "tensor"))
    else:
        axes, grid = ("dp",), mesh
    rows = P((*axes, "tensor"), None)
    in_out = [P(axes, "tensor")] * 3 + [P(axes, None, "tensor")] * 3 + [P("tensor", axes)] * 3
    in_out += [P(axes, None, "tensor")] * 3 + [P("tensor", axes)] * 3 + [P()] * 6
    return jax.shard_map(
        functools.partial(on_device, axes),
        mesh=grid,
        in_specs=(rows, rows, P(axes), *in_out),
        out_specs=(rows, rows, *in_out),
        check_vma=False,
    )
```
